256 devices in a mesh: section: 8 (over z_lo, core), dp: 32 (over y, x, z_hi).
Axes of the slice: x: 4, y: 4, z: 8 (z_hi: 2, z_lo: 4; z = z_hi * 4 + z_lo), core: 2. Of those that a mesh axis runs over, the one named last changes fastest.
Arguments:
- byte_ids: int32 [2, 8192, 8], P(None, 'dp'), may hold values from 0 to 255
- patch_len: int32 [2, 8192], P(None, 'dp'), may hold values from 1 to 8
- table: bfloat16 [256, 4096], replicated, may hold values from -12 to 12
- basis: bfloat16 [4096, 256], replicated, may hold values from -0.09375 to 0.09375
- w_down: bfloat16 [8, 4096, 256], P('section'), may hold values from -0.09375 to 0.09375
- w_up: bfloat16 [8, 4096, 256], P('section'), may hold values from -0.375 to 0.375
- dcoef: bfloat16 [2, 8192, 256], P(None, 'dp'), may hold values from -0.046875 to 0.046875
Outputs:
- grad_down: bfloat16 [8, 4096, 256], P('section')
The draws below stay inside these ranges and needn't reach their ends.
Inputs may be any that keep to these rules, and one draw needn't show every extreme that they name: `byte_ids`: slots at or past a patch's length are ignored.
All inputs are finite; a program needn't handle non-finite values.
Results may differ from the reference program's by a relative error of at most 0.035.
Values may be sent and summed in bfloat16 or wider, within the bound.
A program may use at most 128 MiB of HBM per device.

```python
import jax
import jax.numpy as jnp
from jax import lax

D = 4096
R = 256
K = 256
BYTES = 256
MAXB = 8
MB = 2
PATCH_DEV = 256
PATCHES = 8192
N_SECTION = 8
N_DP = 32


def place_ends(array, own_key, least, largest):
    dims = array.shape
    place = [jax.random.randint(jax.random.fold_in(own_key, axis), (), 0, dims[axis]) for axis in range(len(dims))]
    array = array.at[tuple(place)].set(least)
    longest = dims.index(max(dims))
    place[longest] = (place[longest] + 1) % dims[longest]
    return array.at[tuple(place)].set(largest)


def level_of(key, extent, split, smallest, largest):
    factor_of, own = 1.0, jax.random.fold_in(key, 6)
    for axis_at, parts in split:
        draws = jnp.exp(jax.random.uniform(jax.random.fold_in(own, axis_at), (parts,), jnp.float32, smallest / len(split), largest / len(split)))
        factor_of = factor_of * jnp.repeat(draws, extent[axis_at] // parts).reshape([-1 if axis == axis_at else 1 for axis in range(len(extent))])
    return factor_of


def scatter_about(rng, dims, spread, limit, split=(), kind=jnp.bfloat16):
    array = spread * jax.random.normal(rng, dims, jnp.float32)
    if split:
        array = array * level_of(rng, dims, split, -0.22, 0.18)
    return jnp.clip(array, -limit, limit).astype(kind)


def setup_inputs(seed: int = 0) -> dict:
    key_list = jax.random.split(jax.random.key(seed), 8)
    byte_ids = place_ends(jax.random.randint(key_list[0], (MB, PATCHES, MAXB), 0, BYTES), jax.random.fold_in(key_list[0], 1), 0, BYTES - 1).astype(jnp.int32)
    patch_len = place_ends(jax.random.randint(key_list[1], (MB, PATCHES), 1, MAXB + 1), jax.random.fold_in(key_list[1], 1), 1, MAXB).astype(jnp.int32)
    table = scatter_about(key_list[2], (BYTES, D), 2.0, 12.0)
    basis = scatter_about(key_list[3], (D, R), D ** -0.5, 0.09375)
    w_down = scatter_about(key_list[4], (N_SECTION, D, K), D ** -0.5, 0.09375, ((0, 8),))
    w_up = scatter_about(key_list[5], (N_SECTION, D, K), K ** -0.5, 0.375, ((0, 8),))
    dcoef = scatter_about(key_list[6], (MB, PATCHES, R), ((MB * PATCHES) ** -0.5), 0.046875, ((1, 32),))
    return {"byte_ids": byte_ids, "patch_len": patch_len, "table": table, "basis": basis, "w_down": w_down, "w_up": w_up, "dcoef": dcoef}


def embed_batch(byte_ids, patch_len, table):
    slots = lax.broadcasted_iota(jnp.int32, byte_ids.shape, 1)
    live = slots < patch_len[:, None]
    codes = lax.broadcasted_iota(jnp.int32, (1, 1, table.shape[0]), 2)
    counts = lax.optimization_barrier(jnp.sum(jnp.where((byte_ids[:, :, None] == codes) & live[:, :, None], 1.0, 0.0), axis=1))
    summed = jnp.dot(counts.astype(jnp.bfloat16), table, preferred_element_type=jnp.float32)
    pre = summed * lax.rsqrt(patch_len.astype(jnp.float32))[:, None]
    return jax.nn.silu(pre).astype(jnp.bfloat16)

def forward_section(coefs, anchor, basis, weight_down, weight_up):
    xfull = anchor.astype(jnp.float32) + jnp.dot(coefs, basis.T, preferred_element_type=jnp.float32)
    scale = lax.rsqrt(lax.optimization_barrier(jnp.mean(xfull * xfull, axis=-1, keepdims=True)) + 1e-06)
    normed = (xfull * scale).astype(jnp.bfloat16)
    zvalue = jnp.dot(normed, weight_down, preferred_element_type=jnp.float32)
    active = jax.nn.silu(zvalue).astype(jnp.bfloat16)
    branch = jnp.dot(active, weight_up.T, preferred_element_type=jnp.float32).astype(jnp.bfloat16)
    outputs = (coefs.astype(jnp.float32) + jnp.dot(branch, basis, preferred_element_type=jnp.float32)).astype(jnp.bfloat16)
    return (outputs, xfull, normed, zvalue)

def backward_section(upstream, xfull, zvalue, basis, weight_down, weight_up):
    scale = lax.rsqrt(lax.optimization_barrier(jnp.mean(xfull * xfull, axis=-1, keepdims=True)) + 1e-06)
    grad_branch = jnp.dot(upstream, basis.T, preferred_element_type=jnp.float32).astype(jnp.bfloat16)
    grad_active = jnp.dot(grad_branch, weight_up, preferred_element_type=jnp.float32)
    sigma = jax.nn.sigmoid(zvalue)
    grad_z = (grad_active * sigma * (1.0 + zvalue * (1.0 - sigma))).astype(jnp.bfloat16)
    grad_normed = jnp.dot(grad_z, weight_down.T, preferred_element_type=jnp.float32)
    hfloat = xfull * scale
    grad_x = (scale * (grad_normed - hfloat * lax.optimization_barrier(jnp.mean(grad_normed * hfloat, axis=-1, keepdims=True)))).astype(jnp.bfloat16)
    previous = (upstream.astype(jnp.float32) + jnp.dot(grad_x, basis, preferred_element_type=jnp.float32)).astype(jnp.bfloat16)
    return (previous, grad_z)

def shard_rows(stacked):
    width = stacked.shape[-1]
    shaped = stacked.reshape(MB, N_DP, PATCH_DEV, width)
    return jnp.transpose(shaped, (1, 0, 2, 3)).reshape(N_DP, MB * PATCH_DEV, width)

def partial_product(pieces):
    left, right = pieces
    return jnp.dot(left.T, right, preferred_element_type=jnp.float32).astype(jnp.bfloat16)

def reduce_partials(left, right):
    partials = lax.map(partial_product, (shard_rows(left), shard_rows(right)))
    return lax.optimization_barrier(jnp.sum(partials.astype(jnp.float32), axis=0)).astype(jnp.bfloat16)

def reference(byte_ids, patch_len, table, basis, w_down, w_up, dcoef):
    anchors = [embed_batch(byte_ids[batch_no], patch_len[batch_no], table) for batch_no in range(MB)]
    coef_list = [jnp.zeros((PATCHES, R), jnp.bfloat16) for batch_no in range(MB)]
    section_inputs = []
    for section_no in range(N_SECTION):
        section_inputs.append(list(coef_list))
        coef_list = [forward_section(coef_list[batch_no], anchors[batch_no], basis, w_down[section_no], w_up[section_no])[0] for batch_no in range(MB)]
    upstream = [dcoef[batch_no] for batch_no in range(MB)]
    down_list = [None] * N_SECTION
    for section_no in reversed(range(N_SECTION)):
        normed_all, gradz_all = ([], [])
        for batch_no in range(MB):
            outputs, xfull, normed, zvalue = forward_section(section_inputs[section_no][batch_no], anchors[batch_no], basis, w_down[section_no], w_up[section_no])
            previous, grad_z = backward_section(upstream[batch_no], xfull, zvalue, basis, w_down[section_no], w_up[section_no])
            upstream[batch_no] = previous
            normed_all.append(normed)
            gradz_all.append(grad_z)
        down_list[section_no] = reduce_partials(jnp.stack(normed_all), jnp.stack(gradz_all))
    return jnp.stack(down_list)
```

```python
import functools

import jax
import jax.numpy as jnp
from jax import lax
from jax.experimental import pallas as pl
from jax.experimental.pallas import tpu as pltpu
from jax.sharding import PartitionSpec as P

MESH = pl.DeviceIdType.MESH
RING = 4
F32, BF16 = jnp.float32, jnp.bfloat16


def dot(a, b, dims=((1,), (0,))):
    return lax.dot_general(a, b, (dims, ((), ())), preferred_element_type=F32)


def sigmoid(v):
    return 0.5 + 0.5 * jnp.tanh(0.5 * v)


def kernel(
    ids_ref, table_hbm, basis_hbm, down_hbm, up_hbm, dcoef_ref, out_hbm,
    table, basis, down, up, emb, emb_t, part, res,
    acc_s, acc_e, counts, gram, shared, own_e, all_e,
    z_st, xb_st, r_st, c_out, d_out, c_in, d_in, small,
    big_in, mid_in, z_in, mid,
    load_sem, mu_s, mu_r, e_s, e_r, c_s, c_r, d_s, d_r, ar_s, ar_r, st_sem,
):
    sections = all_e.shape[0]
    me = lax.axis_index("section")
    dp = lax.axis_index("dp")
    zh = lax.rem(dp, 2)
    cx = lax.rem(dp // 2, RING)
    cy = dp // (2 * RING)
    width, rank = basis.shape
    rows = emb.shape[0]
    mine = rows // sections
    tiles = load_sem.shape[1]
    tile = width // tiles

    def copy_to(src, dst, ssem, rsem, where):
        return pltpu.make_async_remote_copy(
            src_ref=src, dst_ref=dst, send_sem=ssem, recv_sem=rsem,
            device_id=where, device_id_type=MESH,
        )

    def others():
        for off in range(1, sections):
            yield lax.rem(me + off, sections)

    def at(x, y, z):
        return {"dp": (y * RING + x) * 2 + z}

    def up1(v):
        return lax.rem(v + 1, RING)

    def dn1(v):
        return lax.rem(v + RING - 1, RING)

    def opp(v):
        return lax.rem(v + 2, RING)

    def load(n, i):
        src = (basis_hbm, down_hbm, up_hbm, table_hbm)[n]
        dst = (basis, down, up, table)[n]
        sl = pl.ds(pl.multiple_of(i * tile, tile), tile)
        if n == 3:
            return pltpu.make_async_copy(src.at[:, sl], dst.at[:, sl], load_sem.at[n, i])
        return pltpu.make_async_copy(src.at[sl, :], dst.at[sl, :], load_sem.at[n, i])

    for i in range(tiles):
        for n in range(3):
            load(n, i).start()
    for i in range(tiles):
        load(3, i).start()

    barrier = pltpu.get_barrier_semaphore()
    for t in others():
        pl.semaphore_signal(barrier, inc=1, device_id={"section": t}, device_id_type=MESH)
    mates = [
        at(up1(cx), cy, zh), at(dn1(cx), cy, zh), at(cx, up1(cy), zh), at(cx, dn1(cy), zh),
        at(cx, cy, 1 - zh),
    ]
    for mate in mates:
        pl.semaphore_signal(barrier, inc=1, device_id=mate, device_id_type=MESH)

    acc_s[...] = jnp.zeros_like(acc_s)

    @pl.loop(0, tiles)
    def _(i):
        for n in range(3):
            load(n, i).wait()
        sl = pl.ds(pl.multiple_of(i * tile, tile), tile)
        bt = basis[sl, :].T
        acc_s[0] += dot(bt, basis[sl, :])
        acc_s[1] += dot(bt, down[sl, :])
        acc_s[2] += dot(bt, up[sl, :])

    gram[...] = acc_s[0].astype(BF16)
    shared[pl.ds(me, 1), 0] = acc_s[1].astype(BF16)[None]
    shared[pl.ds(me, 1), 1] = acc_s[2].astype(BF16)[None]

    pl.semaphore_wait(barrier, sections - 1 + len(mates))

    def share(t):
        return copy_to(shared.at[me], shared.at[me], mu_s.at[t], mu_r.at[me], {"section": t})

    for t in others():
        share(t).start()

    codes = lax.broadcasted_iota(jnp.int32, (rows, table.shape[0]), 1)
    total = jnp.zeros(codes.shape, F32)
    for j in range(ids_ref.shape[1]):
        total += jnp.where(ids_ref[:, j : j + 1] == codes, 1.0, 0.0)
    counts[...] = total.astype(BF16)
    small[...] = lax.rsqrt(jnp.sum(total, axis=1, keepdims=True))
    acc_e[...] = jnp.zeros_like(acc_e)
    step = rows // 4

    @pl.loop(0, tiles)
    def _(i):
        load(3, i).wait()
        sl = pl.ds(pl.multiple_of(i * tile, tile), tile)
        for q in range(4):
            rs = slice(q * step, (q + 1) * step)
            pre = dot(counts[rs, :], table[:, sl]) * small[rs, :]
            anchor = (pre * sigmoid(pre)).astype(BF16)
            emb[rs, sl] = anchor
            acc_e[rs, :] += dot(anchor, down[sl, :])

    own_e[...] = acc_e[...].astype(BF16)

    def slot(t):
        return pl.ds(pl.multiple_of(t * mine, mine), mine)

    def give_e(t):
        return copy_to(own_e.at[slot(t)], all_e.at[me], e_s.at[t], e_r.at[me], {"section": t})

    for t in others():
        give_e(t).start()
    all_e[pl.ds(me, 1)] = own_e[slot(me), :][None]

    fb = jnp.zeros((mine, rank), F32)
    e2 = jnp.zeros((mine, 1), F32)
    for i in range(tiles):
        piece = emb[slot(me), i * tile : (i + 1) * tile]
        fb += dot(piece, basis[i * tile : (i + 1) * tile, :])
        wide = piece.astype(F32)
        e2 += jnp.sum(wide * wide, axis=1, keepdims=True)

    @pl.loop(0, tiles)
    def _(i):
        sl = pl.ds(pl.multiple_of(i * tile, tile), tile)
        for q in range(4):
            rs = slice(q * step, (q + 1) * step)
            emb_t[sl, rs] = emb[rs, sl].T

    def give_c(s):
        return copy_to(c_out.at[s], c_in.at[slot(me)], c_s.at[s], c_r.at[me], {"section": s})

    def give_d(s):
        return copy_to(d_out.at[s], d_in.at[slot(me)], d_s.at[s], d_r.at[me], {"section": s})

    inv = 1.0 / width
    coef = jnp.zeros((mine, rank), F32)
    for s in range(sections):

        @pl.when(me != s)
        def _():
            copy_to(own_e.at[slot(s)], all_e.at[s], e_s.at[s], e_r.at[s], {"section": s}).wait_recv()
            copy_to(shared.at[s], shared.at[s], mu_s.at[s], mu_r.at[s], {"section": s}).wait_recv()

        cb = coef.astype(BF16)
        c_out[s] = cb

        @pl.when(me != s)
        def _():
            give_c(s).start()

        zin = all_e[s].astype(F32)
        xb = fb
        sq = e2
        if s > 0:
            zin = zin + dot(cb, shared[s, 0])
            cg = dot(cb, gram[...])
            xb = xb + cg
            sq = sq + jnp.sum(coef * (fb + xb), axis=1, keepdims=True)
        r = lax.rsqrt(jnp.maximum(sq, 0.0) * inv + 1e-06)
        z = r * zin
        z_st[s] = z
        xb_st[s] = xb
        r_st[s] = r
        act = (z * sigmoid(z)).astype(BF16)
        if s < sections - 1:
            coef = coef + dot(act, shared[s, 1], ((1,), (1,)))

    grad = dcoef_ref[slot(me), :].astype(F32)
    for s in reversed(range(sections)):
        da = dot(grad.astype(BF16), shared[s, 1])
        z = z_st[s]
        r = r_st[s]
        sig = sigmoid(z)
        dz = da * sig * (1.0 + z * (1.0 - sig))
        d_out[s] = (r * dz).astype(BF16)

        @pl.when(me != s)
        def _():
            give_d(s).start()

        if s > 0:
            mean = jnp.sum(dz * z, axis=1, keepdims=True) * inv
            back = dot(dz.astype(BF16), shared[s, 0], ((1,), (1,)))
            grad = grad + r * (back - (r * mean) * xb_st[s])

    c_in[slot(me), :] = c_out[pl.ds(me, 1)][0]
    d_in[slot(me), :] = d_out[pl.ds(me, 1)][0]
    for t in others():
        copy_to(c_out.at[t], c_in.at[slot(t)], c_s.at[t], c_r.at[t], {"section": t}).wait_recv()
        copy_to(d_out.at[t], d_in.at[slot(t)], d_s.at[t], d_r.at[t], {"section": t}).wait_recv()
    for t in others():
        share(t).wait_send()
        give_e(t).wait_send()
        give_c(t).wait_send()
        give_d(t).wait_send()

    gram[...] = dot(c_in[...].T, d_in[...]).astype(BF16)
    piece_rows = width // 16

    @pl.loop(0, 16)
    def _(i):
        sl = pl.ds(pl.multiple_of(i * piece_rows, piece_rows), piece_rows)
        part[sl, :] = (dot(emb_t[sl, :], d_in[...]) + dot(basis[sl, :], gram[...])).astype(BF16)

    half, b1, b2 = width // 2, width // 8, width // 32
    first = [cx, cy]
    second = [cy, cx]

    def along(h, stage, v):
        if (h == 0) == (stage == 0):
            return at(v, cy, zh)
        return at(cx, v, zh)

    def rows_at(start, size):
        return pl.ds(pl.multiple_of(start, size), size)

    def add_into(dst, dst_rows, *others_):
        total_ = dst[dst_rows, :].astype(F32)
        for o in others_:
            total_ += o.astype(F32)
        dst[dst_rows, :] = total_.astype(BF16)

    def scatter(h, stage):
        if stage == 0:
            buf, base, size, pos, land = part, h * half, b1, first[h], big_in
        else:
            buf, base, size, pos, land = mid.at[h], 0, b2, second[h], mid_in
        hf = size // 2
        n0 = h * 21 + stage * 6
        right, left, far = up1(pos), dn1(pos), opp(pos)

        def blk(owner, part_no):
            return rows_at(base + owner * size + part_no * hf, hf)

        def cp(k, owner, part_no, to):
            return copy_to(
                buf.at[blk(owner, part_no)], land.at[h, k], ar_s.at[n0 + k], ar_r.at[n0 + k],
                along(h, stage, to),
            )

        moves = [
            cp(0, far, 0, right), cp(1, far, 1, left), cp(2, right, 1, right),
            cp(3, left, 0, left), cp(4, right, 0, right), cp(5, left, 1, left),
        ]

        def begin():
            for k in range(4):
                moves[k].start()

        def middle():
            moves[0].wait_recv()
            add_into(buf, blk(right, 0), land[h, 0])
            moves[4].start()
            moves[1].wait_recv()
            add_into(buf, blk(left, 1), land[h, 1])
            moves[5].start()

        def end(dst, dst_row):
            moves[3].wait_recv()
            moves[4].wait_recv()
            dst[dst_row : dst_row + hf, :] = (
                buf[blk(pos, 0), :].astype(F32) + land[h, 3].astype(F32) + land[h, 4].astype(F32)
            ).astype(BF16)
            moves[2].wait_recv()
            moves[5].wait_recv()
            dst[dst_row + hf : dst_row + size, :] = (
                buf[blk(pos, 1), :].astype(F32) + land[h, 2].astype(F32) + land[h, 5].astype(F32)
            ).astype(BF16)

        def finish():
            for m in moves:
                m.wait_send()

        return begin, middle, end, finish

    def gather(h, stage):
        if stage == 0:
            base, size, pos = h * half, b1, first[h]
        else:
            base, size, pos = h * half + first[h] * b1, b2, second[h]
        hf = size // 2
        n0 = h * 21 + 13 + stage * 4
        right, left = up1(pos), dn1(pos)

        def cp(k, owner, off, n, to):
            sl = rows_at(base + owner * size + off, n)
            return copy_to(
                res.at[sl], res.at[sl], ar_s.at[n0 + k], ar_r.at[n0 + k], along(h, stage, to)
            )

        moves = [
            cp(0, pos, 0, size, right), cp(1, pos, 0, size, left),
            cp(2, left, 0, hf, right), cp(3, right, hf, hf, left),
        ]

        def begin():
            moves[0].start()
            moves[1].start()

        def middle():
            moves[0].wait_recv()
            moves[2].start()
            moves[1].wait_recv()
            moves[3].start()

        def end():
            moves[2].wait_recv()
            moves[3].wait_recv()

        def finish():
            for m in moves:
                m.wait_send()

        return begin, middle, end, finish

    rs1 = [scatter(h, 0) for h in range(2)]
    rs2 = [scatter(h, 1) for h in range(2)]
    ag2 = [gather(h, 1) for h in range(2)]
    ag1 = [gather(h, 0) for h in range(2)]
    for h in range(2):
        rs1[h][0]()
    for h in range(2):
        rs1[h][1]()
    for h in range(2):
        rs1[h][2](mid.at[h], 0)
        rs2[h][0]()
    for h in range(2):
        rs2[h][1]()
    swaps = []
    for h in range(2):
        rs2[h][2](mid.at[h], 4 * b2)
        swap = copy_to(
            mid.at[h, pl.ds(4 * b2, b2)], z_in.at[h], ar_s.at[h * 21 + 12], ar_r.at[h * 21 + 12],
            at(cx, cy, 1 - zh),
        )
        swap.start()
        swaps.append(swap)
    for h in range(2):
        swaps[h].wait_recv()
        sl = rows_at(h * half + first[h] * b1 + second[h] * b2, b2)
        res[sl, :] = (mid[h, 4 * b2 :, :].astype(F32) + z_in[h].astype(F32)).astype(BF16)
        ag2[h][0]()
    for h in range(2):
        ag2[h][1]()
    for h in range(2):
        ag2[h][2]()
        ag1[h][0]()
    for h in range(2):
        ag1[h][1]()
    for h in range(2):
        ag1[h][2]()
    store = pltpu.make_async_copy(res, out_hbm, st_sem)
    store.start()
    for h in range(2):
        for g in (rs1, rs2, ag2, ag1):
            g[h][3]()
        swaps[h].wait_send()
    store.wait()


def on_device(byte_ids, patch_len, table, basis, w_down, w_up, dcoef):
    sections = lax.axis_size("section")
    batches, here, slots = byte_ids.shape
    rows = batches * here
    width, rank = basis.shape
    hidden = w_down.shape[2]
    mine = rows // sections
    tiles = 8
    live = lax.broadcasted_iota(jnp.int32, byte_ids.shape, 2) < patch_len[:, :, None]
    ids = jnp.where(live, byte_ids, -1).reshape(rows, slots)
    half, b1, b2 = width // 2, width // 8, width // 32
    vmem = pl.BlockSpec(memory_space=pltpu.VMEM)
    hbm = pl.BlockSpec(memory_space=pl.ANY)
    dma = pltpu.SemaphoreType.DMA
    scratch = [
        pltpu.VMEM((table.shape[0], width), BF16),
        pltpu.VMEM((width, rank), BF16),
        pltpu.VMEM((width, hidden), BF16),
        pltpu.VMEM((width, hidden), BF16),
        pltpu.VMEM((rows, width), BF16),
        pltpu.VMEM((width, rows), BF16),
        pltpu.VMEM((width, hidden), BF16),
        pltpu.VMEM((width, hidden), BF16),
        pltpu.VMEM((3, rank, hidden), F32),
        pltpu.VMEM((rows, hidden), F32),
        pltpu.VMEM((rows, table.shape[0]), BF16),
        pltpu.VMEM((rank, hidden), BF16),
        pltpu.VMEM((sections, 2, rank, hidden), BF16),
        pltpu.VMEM((rows, hidden), BF16),
        pltpu.VMEM((sections, mine, hidden), BF16),
        pltpu.VMEM((sections, mine, hidden), F32),
        pltpu.VMEM((sections, mine, rank), F32),
        pltpu.VMEM((sections, mine, 1), F32),
        pltpu.VMEM((sections, mine, rank), BF16),
        pltpu.VMEM((sections, mine, hidden), BF16),
        pltpu.VMEM((rows, rank), BF16),
        pltpu.VMEM((rows, hidden), BF16),
        pltpu.VMEM((rows, 1), F32),
        pltpu.VMEM((2, 6, b1 // 2, hidden), BF16),
        pltpu.VMEM((2, 6, b2 // 2, hidden), BF16),
        pltpu.VMEM((2, b2, hidden), BF16),
        pltpu.VMEM((2, b1 + b2, hidden), BF16),
        dma((4, tiles)),
        dma((sections,)), dma((sections,)), dma((sections,)), dma((sections,)),
        dma((sections,)), dma((sections,)), dma((sections,)), dma((sections,)),
        dma((42,)), dma((42,)), dma,
    ]
    out = pl.pallas_call(
        kernel,
        out_shape=jax.ShapeDtypeStruct((width, hidden), BF16),
        in_specs=[vmem, hbm, hbm, hbm, hbm, vmem],
        out_specs=hbm,
        scratch_shapes=scratch,
        compiler_params=pltpu.CompilerParams(
            collective_id=0, has_side_effects=True, vmem_limit_bytes=56 * 1024 * 1024
        ),
    )(ids, table, basis, w_down[0], w_up[0], dcoef.reshape(rows, rank))
    return out[None]


def solution(mesh):
    return jax.shard_map(
        on_device,
        mesh=mesh,
        in_specs=(
            P(None, "dp", None),
            P(None, "dp"),
            P(),
            P(),
            P("section", None, None),
            P("section", None, None),
            P(None, "dp", None),
        ),
        out_specs=P("section", None, None),
        check_vma=False,
    )
```

```python
import functools

import jax
import jax.numpy as jnp
from jax import lax
from jax.experimental import pallas as pl
from jax.experimental.pallas import tpu as pltpu
from jax.sharding import PartitionSpec as P

MESH = pl.DeviceIdType.MESH
RING = 4
F32, BF16 = jnp.float32, jnp.bfloat16
STREAMS = 4
TIMES = {
    4: ((0, 4.2, 8.4, 13, 18.5, 23, 28, 32), (1, 2.8, 2.8, 2.8, 2.8, 2.8, 2.8, 2.8)),
    8: ((0, 3.5, 7, 11.2, 16.7, 21, 25, 28.5), (0.6, 1.4, 1.4, 1.4, 1.4, 1.4, 1.4, 1.6)),
}


def dot(a, b, dims=((1,), (0,))):
    return lax.dot_general(a, b, (dims, ((), ())), preferred_element_type=F32)


def sigmoid(v):
    return 0.5 + 0.5 * jnp.tanh(0.5 * v)


def kernel(
    streams, times,
    ids_ref, table_hbm, basis_hbm, down_hbm, up_hbm, dcoef_ref, out_hbm,
    table, basis, down, up, emb, emb_t, part, res,
    acc_s, acc_e, counts, gram, shared, own_e, all_e,
    z_st, xb_st, r_st, c_out, d_out, c_in, d_in, small, hop_out, hop_in,
    big_in, mid, mid_in, z_in,
    load_sem, mu_s, mu_r, e_s, e_r, c_s, c_r, d_s, d_r, hop_s, hop_r, ar_s, ar_r, st_sem,
):
    sections = lax.axis_size("section")
    group = all_e.shape[0]
    me = lax.axis_index("section")
    dp = lax.axis_index("dp")
    zh = lax.rem(dp, 2)
    cx = lax.rem(dp // 2, RING)
    cy = dp // (2 * RING)
    width, rank = basis.shape
    rows = emb.shape[0]
    mine = rows // group
    tiles = load_sem.shape[1]
    tile = width // tiles
    side = me // group
    here = lax.rem(me, group)
    partner = lax.rem(me + group, sections)

    def copy_to(src, dst, ssem, rsem, where):
        return pltpu.make_async_remote_copy(
            src_ref=src, dst_ref=dst, send_sem=ssem, recv_sem=rsem,
            device_id=where, device_id_type=MESH,
        )

    def others():
        for off in range(1, group):
            yield lax.rem(here + off, group)

    def device(t):
        return {"section": side * group + t}

    def at(x, y, z):
        return {"dp": (y * RING + x) * 2 + z}

    def turn(v, k):
        return lax.rem(v + k, RING)

    def load(n, i):
        src = (basis_hbm, down_hbm, up_hbm, table_hbm)[n]
        dst = (basis, down, up, table)[n]
        sl = pl.ds(pl.multiple_of(i * tile, tile), tile)
        if n == 3:
            return pltpu.make_async_copy(src.at[:, sl], dst.at[:, sl], load_sem.at[n, i])
        return pltpu.make_async_copy(src.at[sl, :], dst.at[sl, :], load_sem.at[n, i])

    for i in range(tiles):
        for n in range(3):
            load(n, i).start()
    for i in range(tiles):
        load(3, i).start()

    barrier = pltpu.get_barrier_semaphore()
    mates = [device(t) for t in others()] + [{"section": partner}]
    mates += [at(turn(cx, k), cy, zh) for k in range(1, RING)]
    mates += [at(cx, turn(cy, k), zh) for k in range(1, RING)]
    mates += [at(cx, cy, 1 - zh)]
    for mate in mates:
        pl.semaphore_signal(barrier, inc=1, device_id=mate, device_id_type=MESH)

    acc_s[...] = jnp.zeros_like(acc_s)

    @pl.loop(0, tiles)
    def _(i):
        for n in range(3):
            load(n, i).wait()
        sl = pl.ds(pl.multiple_of(i * tile, tile), tile)
        bt = basis[sl, :].T
        acc_s[0] += dot(bt, basis[sl, :])
        acc_s[1] += dot(bt, down[sl, :])
        acc_s[2] += dot(bt, up[sl, :])

    gram[...] = acc_s[0].astype(BF16)
    shared[pl.ds(here, 1), 0] = acc_s[1].astype(BF16)[None]
    shared[pl.ds(here, 1), 1] = acc_s[2].astype(BF16)[None]

    pl.semaphore_wait(barrier, len(mates))

    twin = here + 1 - 2 * lax.rem(here, 2)
    far = lax.rem(here + 2, group)
    far_twin = lax.rem(twin + 2, group)

    def share(k, what, to):
        return copy_to(shared.at[what], shared.at[what], mu_s.at[k], mu_r.at[k], device(to))

    share(1, here, far).start()
    share(0, here, twin).start()

    codes = lax.broadcasted_iota(jnp.int32, (rows, table.shape[0]), 1)
    total = jnp.zeros(codes.shape, F32)
    for j in range(ids_ref.shape[1]):
        total += jnp.where(ids_ref[:, j : j + 1] == codes, 1.0, 0.0)
    counts[...] = total.astype(BF16)
    small[...] = lax.rsqrt(jnp.sum(total, axis=1, keepdims=True))
    acc_e[...] = jnp.zeros_like(acc_e)
    step = rows // 4

    @pl.loop(0, tiles)
    def _(i):
        load(3, i).wait()
        sl = pl.ds(pl.multiple_of(i * tile, tile), tile)
        for q in range(4):
            rs = slice(q * step, (q + 1) * step)
            pre = dot(counts[rs, :], table[:, sl]) * small[rs, :]
            anchor = (pre * sigmoid(pre)).astype(BF16)
            emb[rs, sl] = anchor
            acc_e[rs, :] += dot(anchor, down[sl, :])

    own_e[...] = acc_e[...].astype(BF16)

    def slot(t):
        return pl.ds(pl.multiple_of(t * mine, mine), mine)

    def give_e(t):
        return copy_to(own_e.at[slot(t)], all_e.at[here], e_s.at[t], e_r.at[here], device(t))

    for t in others():
        give_e(t).start()
    all_e[pl.ds(here, 1)] = own_e[slot(here), :][None]

    fb = jnp.zeros((mine, rank), F32)
    e2 = jnp.zeros((mine, 1), F32)
    for i in range(tiles):
        piece = emb[slot(here), i * tile : (i + 1) * tile]
        fb += dot(piece, basis[i * tile : (i + 1) * tile, :])
        wide = piece.astype(F32)
        e2 += jnp.sum(wide * wide, axis=1, keepdims=True)

    share(1, far, far).wait_recv()
    share(2, far, twin).start()

    @pl.loop(0, tiles)
    def _(i):
        sl = pl.ds(pl.multiple_of(i * tile, tile), tile)
        for q in range(4):
            rs = slice(q * step, (q + 1) * step)
            emb_t[sl, rs] = emb[rs, sl].T

    share(0, twin, twin).wait_recv()
    share(2, far_twin, twin).wait_recv()
    for t in others():
        copy_to(own_e.at[slot(t)], all_e.at[t], e_s.at[t], e_r.at[t], device(t)).wait_recv()

    def give_c(t):
        return copy_to(c_out.at[t], c_in.at[slot(here)], c_s.at[t], c_r.at[here], device(t))

    def give_d(t):
        return copy_to(d_out.at[t], d_in.at[slot(here)], d_s.at[t], d_r.at[here], device(t))

    def hop(k):
        return copy_to(hop_out.at[k], hop_in.at[k], hop_s.at[k], hop_r.at[k], {"section": partner})

    inv = 1.0 / width

    @pl.when(side == 0)
    def _():
        hop_in[0] = jnp.zeros(hop_in.shape[1:], BF16)

    @pl.when(side == 1)
    def _():
        hop(0).wait_recv()

    coef = hop_in[0].astype(F32)
    for s in range(group):
        cb = coef.astype(BF16)
        c_out[s] = cb

        @pl.when(here != s)
        def _():
            give_c(s).start()

        cg = dot(cb, gram[...])
        xb = fb + cg
        sq = e2 + jnp.sum(coef * (fb + xb), axis=1, keepdims=True)
        r = lax.rsqrt(jnp.maximum(sq, 0.0) * inv + 1e-06)
        z = r * (all_e[s].astype(F32) + dot(cb, shared[s, 0]))
        z_st[s] = z
        xb_st[s] = xb
        r_st[s] = r
        act = (z * sigmoid(z)).astype(BF16)
        coef = coef + dot(act, shared[s, 1], ((1,), (1,)))

    @pl.when(side == 0)
    def _():
        hop_out[0] = coef.astype(BF16)
        hop(0).start()
        hop(1).wait_recv()

    @pl.when(side == 1)
    def _():
        hop_in[1] = dcoef_ref[slot(here), :]

    grad = hop_in[1].astype(F32)
    for s in reversed(range(group)):
        da = dot(grad.astype(BF16), shared[s, 1])
        z = z_st[s]
        r = r_st[s]
        sig = sigmoid(z)
        dz = da * sig * (1.0 + z * (1.0 - sig))
        d_out[s] = (r * dz).astype(BF16)

        @pl.when(here != s)
        def _():
            give_d(s).start()

        mean = jnp.sum(dz * z, axis=1, keepdims=True) * inv
        back = dot(dz.astype(BF16), shared[s, 0], ((1,), (1,)))
        grad = grad + r * (back - (r * mean) * xb_st[s])

    @pl.when(side == 1)
    def _():
        hop_out[1] = grad.astype(BF16)
        hop(1).start()

    c_in[slot(here), :] = c_out[pl.ds(here, 1)][0]
    d_in[slot(here), :] = d_out[pl.ds(here, 1)][0]
    for t in others():
        copy_to(c_out.at[t], c_in.at[slot(t)], c_s.at[t], c_r.at[t], device(t)).wait_recv()
        copy_to(d_out.at[t], d_in.at[slot(t)], d_s.at[t], d_r.at[t], device(t)).wait_recv()

    gram[...] = dot(c_in[...].T, d_in[...]).astype(BF16)
    own = width // streams
    b1, b2 = own // RING, own // RING // RING
    hf = b1 // 2
    per = 17

    def rows_at(start, size):
        return pl.ds(pl.multiple_of(start, size), size)

    def along(st, stage, v):
        if st % 2 == stage:
            return at(v, cy, zh)
        return at(cx, v, zh)

    def add(*parts):
        total_ = parts[0].astype(F32)
        for p in parts[1:]:
            total_ += p.astype(F32)
        return total_.astype(BF16)

    def stream(st):
        base = st * own
        pos, pos2 = (cx, cy) if st % 2 == 0 else (cy, cx)
        right, left, opposite = turn(pos, 1), turn(pos, 3), turn(pos, 2)
        n0 = st * per

        def send(k, src, dst, to):
            return copy_to(src, dst, ar_s.at[n0 + k], ar_r.at[n0 + k], to)

        def blk(owner, part_no):
            return rows_at(base + owner * b1 + part_no * hf, hf)

        def over(k, owner, part_no, to):
            return send(k, part.at[blk(owner, part_no)], big_in.at[st, k], along(st, 0, to))

        scat = [
            over(0, opposite, 0, right), over(1, opposite, 1, left), over(2, right, 1, right),
            over(3, left, 0, left), over(4, right, 0, right), over(5, left, 1, left),
        ]

        def sub(v):
            return rows_at(v * b2, b2)

        scat2 = [
            send(5 + o, mid.at[st, sub(turn(pos2, o))], mid_in.at[st, o - 1],
                 along(st, 1, turn(pos2, o)))
            for o in range(1, RING)
        ]
        swap = send(9, mid.at[st, pl.ds(b1, b2)], z_in.at[st], at(cx, cy, 1 - zh))
        mine_sl = rows_at(base + pos * b1 + pos2 * b2, b2)
        gath2 = [
            send(9 + o, res.at[mine_sl], res.at[mine_sl], along(st, 1, turn(pos2, o)))
            for o in range(1, RING)
        ]

        def whole(k, owner, off, n, to):
            sl = rows_at(base + owner * b1 + off, n)
            return send(13 + k, res.at[sl], res.at[sl], along(st, 0, to))

        gath = [
            whole(0, pos, 0, b1, right), whole(1, pos, 0, b1, left),
            whole(2, left, 0, hf, right), whole(3, right, hf, hf, left),
        ]
        store = pltpu.make_async_copy(
            res.at[pl.ds(base, own)], out_hbm.at[pl.ds(base, own)], st_sem.at[st]
        )

        def product():
            sl = pl.ds(base, own)
            part[sl, :] = (dot(emb_t[sl, :], d_in[...]) + dot(basis[sl, :], gram[...])).astype(BF16)
            for k in range(4):
                scat[k].start()

        def pass_on():
            scat[0].wait_recv()
            part[blk(right, 0), :] = add(part[blk(right, 0), :], big_in[st, 0])
            scat[4].start()
            scat[1].wait_recv()
            part[blk(left, 1), :] = add(part[blk(left, 1), :], big_in[st, 1])
            scat[5].start()

        def block_done():
            scat[3].wait_recv()
            scat[4].wait_recv()
            mid[st, 0:hf, :] = add(part[blk(pos, 0), :], big_in[st, 3], big_in[st, 4])
            scat[2].wait_recv()
            scat[5].wait_recv()
            mid[st, hf:b1, :] = add(part[blk(pos, 1), :], big_in[st, 2], big_in[st, 5])
            for m in scat2:
                m.start()

        def sub_done():
            for m in scat2:
                m.wait_recv()
            mid[st, b1 : b1 + b2, :] = add(
                mid[st, sub(pos2), :], mid_in[st, 0], mid_in[st, 1], mid_in[st, 2]
            )
            swap.start()

        def total_done():
            swap.wait_recv()
            res[mine_sl, :] = add(mid[st, b1 : b1 + b2, :], z_in[st])
            for m in gath2:
                m.start()

        def block_back():
            for m in gath2:
                m.wait_recv()
            gath[0].start()
            gath[1].start()

        def forward():
            gath[0].wait_recv()
            gath[2].start()
            gath[1].wait_recv()
            gath[3].start()

        def out():
            gath[2].wait_recv()
            gath[3].wait_recv()
            store.start()

        def finish():
            for m in scat + scat2 + [swap] + gath2 + gath:
                m.wait_send()
            store.wait()

        return [product, pass_on, block_done, sub_done, total_done, block_back, forward, out], finish

    made = [stream(st) for st in range(streams)]
    order = sorted(
        (times[0][k] + times[1][k] * (st // 2), st, k) for st in range(streams) for k in range(8)
    )
    for _, st, k in order:
        made[st][0][k]()
    for st in range(streams):
        made[st][1]()

    share(1, here, far).wait_send()
    share(0, here, twin).wait_send()
    share(2, far, twin).wait_send()
    for t in others():
        give_e(t).wait_send()
        give_c(t).wait_send()
        give_d(t).wait_send()

    @pl.when(side == 0)
    def _():
        hop(0).wait_send()

    @pl.when(side == 1)
    def _():
        hop(1).wait_send()


def on_device(byte_ids, patch_len, table, basis, w_down, w_up, dcoef):
    sections = lax.axis_size("section")
    batches, here, slots = byte_ids.shape
    rows = batches * here
    width, rank = basis.shape
    hidden = w_down.shape[2]
    group = sections // 2
    mine = rows // group
    tiles = 8
    streams = STREAMS
    live = lax.broadcasted_iota(jnp.int32, byte_ids.shape, 2) < patch_len[:, :, None]
    ids = jnp.where(live, byte_ids, -1).reshape(rows, slots)
    b1 = width // streams // RING
    b2 = b1 // RING
    vmem = pl.BlockSpec(memory_space=pltpu.VMEM)
    hbm = pl.BlockSpec(memory_space=pl.ANY)
    dma = pltpu.SemaphoreType.DMA
    scratch = [
        pltpu.VMEM((table.shape[0], width), BF16),
        pltpu.VMEM((width, rank), BF16),
        pltpu.VMEM((width, hidden), BF16),
        pltpu.VMEM((width, hidden), BF16),
        pltpu.VMEM((rows, width), BF16),
        pltpu.VMEM((width, rows), BF16),
        pltpu.VMEM((width, hidden), BF16),
        pltpu.VMEM((width, hidden), BF16),
        pltpu.VMEM((3, rank, hidden), F32),
        pltpu.VMEM((rows, hidden), F32),
        pltpu.VMEM((rows, table.shape[0]), BF16),
        pltpu.VMEM((rank, hidden), BF16),
        pltpu.VMEM((group, 2, rank, hidden), BF16),
        pltpu.VMEM((rows, hidden), BF16),
        pltpu.VMEM((group, mine, hidden), BF16),
        pltpu.VMEM((group, mine, hidden), F32),
        pltpu.VMEM((group, mine, rank), F32),
        pltpu.VMEM((group, mine, 1), F32),
        pltpu.VMEM((group, mine, rank), BF16),
        pltpu.VMEM((group, mine, hidden), BF16),
        pltpu.VMEM((rows, rank), BF16),
        pltpu.VMEM((rows, hidden), BF16),
        pltpu.VMEM((rows, 1), F32),
        pltpu.VMEM((2, mine, rank), BF16),
        pltpu.VMEM((2, mine, rank), BF16),
        pltpu.VMEM((streams, 6, b1 // 2, hidden), BF16),
        pltpu.VMEM((streams, b1 + b2, hidden), BF16),
        pltpu.VMEM((streams, 3, b2, hidden), BF16),
        pltpu.VMEM((streams, b2, hidden), BF16),
        dma((4, tiles)), dma((3,)), dma((3,)),
        dma((group,)), dma((group,)), dma((group,)), dma((group,)), dma((group,)), dma((group,)),
        dma((2,)), dma((2,)), dma((streams * 17,)), dma((streams * 17,)), dma((streams,)),
    ]
    out = pl.pallas_call(
        functools.partial(kernel, streams, TIMES[streams]),
        out_shape=jax.ShapeDtypeStruct((width, hidden), BF16),
        in_specs=[vmem, hbm, hbm, hbm, hbm, vmem],
        out_specs=hbm,
        scratch_shapes=scratch,
        compiler_params=pltpu.CompilerParams(
            collective_id=0, has_side_effects=True, vmem_limit_bytes=56 * 1024 * 1024
        ),
    )(ids, table, basis, w_down[0], w_up[0], dcoef.reshape(rows, rank))
    return out[None]


def solution(mesh):
    return jax.shard_map(
        on_device,
        mesh=mesh,
        in_specs=(
            P(None, "dp", None),
            P(None, "dp"),
            P(),
            P(),
            P("section", None, None),
            P("section", None, None),
            P(None, "dp", None),
        ),
        out_specs=P("section", None, None),
        check_vma=False,
    )
```

```python
import functools

import jax
import jax.numpy as jnp
from jax import lax
from jax.experimental import pallas as pl
from jax.experimental.pallas import tpu as pltpu
from jax.sharding import PartitionSpec as P

MESH = pl.DeviceIdType.MESH
RING = 4
F32, BF16 = jnp.float32, jnp.bfloat16
STREAMS = 4
TIMES = {
    4: ((0, 4.2, 4.2, 8.4, 13, 18.5, 23, 28, 28, 32), (1, 2.8, 2.8, 2.8, 2.8, 2.8, 2.8, 2.8, 2.8, 2.8)),
}


def dot(a, b, dims=((1,), (0,))):
    return lax.dot_general(a, b, (dims, ((), ())), preferred_element_type=F32)


def sigmoid(v):
    return 0.5 + 0.5 * jnp.tanh(0.5 * v)


def kernel(
    streams, times,
    ids_ref, len_ref, table_hbm, basis_hbm, down_hbm, up_hbm, dcoef_hbm, out_hbm,
    table, basis, down, up, emb, emb_t, part, res,
    acc_s, acc_e, counts, gram, shared, own_e, all_e,
    z_st, xb_st, r_st, c_out, d_out, c_in, d_in, small, hop_out, hop_in,
    big_in, mid, mid_in, z_in,
    load_sem, mu_s, mu_r, e_s, e_r, c_s, c_r, d_s, d_r, hop_s, hop_r, ar_s, ar_r, st_sem,
):
    sections = lax.axis_size("section")
    group = all_e.shape[0]
    me = lax.axis_index("section")
    dp = lax.axis_index("dp")
    zh = lax.rem(dp, 2)
    cx = lax.rem(dp // 2, RING)
    cy = dp // (2 * RING)
    width, rank = basis.shape
    rows = emb.shape[0]
    mine = rows // group
    tiles = load_sem.shape[1]
    tile = width // tiles
    side = me // group
    here = lax.rem(me, group)
    partner = lax.rem(me + group, sections)

    def copy_to(src, dst, ssem, rsem, where):
        return pltpu.make_async_remote_copy(
            src_ref=src, dst_ref=dst, send_sem=ssem, recv_sem=rsem,
            device_id=where, device_id_type=MESH,
        )

    def others():
        for off in range(1, group):
            yield lax.rem(here + off, group)

    def device(t):
        return {"section": side * group + t}

    def at(x, y, z):
        return {"dp": (y * RING + x) * 2 + z}

    def turn(v, k):
        return lax.rem(v + k, RING)

    def load(n, i):
        src = (basis_hbm, down_hbm, up_hbm, table_hbm)[n]
        dst = (basis, down, up, table)[n]
        sl = pl.ds(pl.multiple_of(i * tile, tile), tile)
        if n == 3:
            return pltpu.make_async_copy(src.at[:, sl], dst.at[:, sl], load_sem.at[n, i])
        return pltpu.make_async_copy(src.at[sl, :], dst.at[sl, :], load_sem.at[n, i])

    for i in range(tiles):
        for n in range(3):
            load(n, i).start()
    for i in range(tiles):
        load(3, i).start()

    barrier = pltpu.get_barrier_semaphore()
    mates = [device(t) for t in others()] + [{"section": partner}]
    mates += [at(turn(cx, k), cy, zh) for k in range(1, RING)]
    mates += [at(cx, turn(cy, k), zh) for k in range(1, RING)]
    mates += [at(cx, cy, 1 - zh)]
    for mate in mates:
        pl.semaphore_signal(barrier, inc=1, device_id=mate, device_id_type=MESH)

    acc_s[...] = jnp.zeros_like(acc_s)

    @pl.loop(0, tiles)
    def _(i):
        for n in range(3):
            load(n, i).wait()
        sl = pl.ds(pl.multiple_of(i * tile, tile), tile)
        bt = basis[sl, :].T
        acc_s[0] += dot(bt, basis[sl, :])
        acc_s[1] += dot(bt, down[sl, :])
        acc_s[2] += dot(bt, up[sl, :])

    gram[...] = acc_s[0].astype(BF16)
    shared[pl.ds(here, 1), 0] = acc_s[1].astype(BF16)[None]
    shared[pl.ds(here, 1), 1] = acc_s[2].astype(BF16)[None]

    pl.semaphore_wait(barrier, len(mates))

    twin = here + 1 - 2 * lax.rem(here, 2)
    far = lax.rem(here + 2, group)
    far_twin = lax.rem(twin + 2, group)

    def share(k, what, to):
        return copy_to(shared.at[what], shared.at[what], mu_s.at[k], mu_r.at[k], device(to))

    share(1, here, far).start()
    share(0, here, twin).start()

    batches, slots, here_rows = ids_ref.shape
    codes = lax.broadcasted_iota(jnp.int32, (table.shape[0], here_rows), 0)
    for m in range(batches):
        total = jnp.zeros(codes.shape, F32)
        for j in range(slots):
            live = jnp.where(len_ref[m : m + 1, :] > j, ids_ref[m, j : j + 1, :], -1)
            total += jnp.where(live == codes, 1.0, 0.0)
        total = total.T
        rs = slice(m * here_rows, (m + 1) * here_rows)
        counts[rs, :] = total.astype(BF16)
        small[rs, :] = lax.rsqrt(jnp.sum(total, axis=1, keepdims=True))
    acc_e[...] = jnp.zeros_like(acc_e)
    step = rows // 4

    @pl.loop(0, tiles)
    def _(i):
        load(3, i).wait()
        sl = pl.ds(pl.multiple_of(i * tile, tile), tile)
        for q in range(2):
            rs = slice(q * rows // 2, (q + 1) * rows // 2)
            pre = dot(counts[rs, :], table[:, sl]) * small[rs, :]
            anchor = (pre * sigmoid(pre)).astype(BF16)
            emb[rs, sl] = anchor
            acc_e[rs, :] += dot(anchor, down[sl, :])

    own_e[...] = acc_e[...].astype(BF16)

    def slot(t):
        return pl.ds(pl.multiple_of(t * mine, mine), mine)

    def give_e(t):
        return copy_to(own_e.at[slot(t)], all_e.at[here], e_s.at[t], e_r.at[here], device(t))

    for t in others():
        give_e(t).start()
    all_e[pl.ds(here, 1)] = own_e[slot(here), :][None]

    fb = jnp.zeros((mine, rank), F32)
    e2 = jnp.zeros((mine, 1), F32)
    for i in range(tiles):
        piece = emb[slot(here), i * tile : (i + 1) * tile]
        fb += dot(piece, basis[i * tile : (i + 1) * tile, :])
        wide = piece.astype(F32)
        e2 += jnp.sum(wide * wide, axis=1, keepdims=True)

    share(1, far, far).wait_recv()
    share(2, far, twin).start()

    def flip():
        @pl.loop(0, tiles)
        def _(i):
            sl = pl.ds(pl.multiple_of(i * tile, tile), tile)
            for q in range(4):
                rs = slice(q * step, (q + 1) * step)
                emb_t[sl, rs] = emb[rs, sl].T

    share(0, twin, twin).wait_recv()
    share(2, far_twin, twin).wait_recv()
    for t in others():
        copy_to(own_e.at[slot(t)], all_e.at[t], e_s.at[t], e_r.at[t], device(t)).wait_recv()

    def give_c(t):
        return copy_to(c_out.at[t], c_in.at[slot(here)], c_s.at[t], c_r.at[here], device(t))

    def give_d(t):
        return copy_to(d_out.at[t], d_in.at[slot(here)], d_s.at[t], d_r.at[here], device(t))

    def hop(k):
        return copy_to(hop_out.at[k], hop_in.at[k], hop_s.at[k], hop_r.at[k], {"section": partner})

    inv = 1.0 / width

    @pl.when(side == 0)
    def _():
        hop_in[0] = jnp.zeros(hop_in.shape[1:], BF16)

    @pl.when(side == 1)
    def _():
        flip()
        hop(0).wait_recv()

    coef = hop_in[0].astype(F32)
    for s in range(group):
        cb = coef.astype(BF16)
        c_out[s] = cb
        cg = dot(cb, gram[...])
        xb = fb + cg
        sq = e2 + jnp.sum(coef * (fb + xb), axis=1, keepdims=True)
        r = lax.rsqrt(jnp.maximum(sq, 0.0) * inv + 1e-06)
        z = r * (all_e[s].astype(F32) + dot(cb, shared[s, 0]))
        z_st[s] = z
        xb_st[s] = xb
        r_st[s] = r
        act = (z * sigmoid(z)).astype(BF16)
        coef = coef + dot(act, shared[s, 1], ((1,), (1,)))

    @pl.when(side == 0)
    def _():
        hop_out[0] = coef.astype(BF16)
        hop(0).start()

    for t in others():
        give_c(t).start()

    @pl.when(side == 0)
    def _():
        flip()
        hop(1).wait_recv()

    @pl.when(side == 1)
    def _():
        last = pltpu.make_async_copy(dcoef_hbm.at[slot(here)], hop_in.at[1], st_sem.at[0])
        last.start()
        last.wait()

    grad = hop_in[1].astype(F32)
    for s in reversed(range(group)):
        da = dot(grad.astype(BF16), shared[s, 1])
        z = z_st[s]
        r = r_st[s]
        sig = sigmoid(z)
        dz = da * sig * (1.0 + z * (1.0 - sig))
        d_out[s] = (r * dz).astype(BF16)

        @pl.when((here != s) & (side == 0))
        def _():
            give_d(s).start()

        mean = jnp.sum(dz * z, axis=1, keepdims=True) * inv
        back = dot(dz.astype(BF16), shared[s, 0], ((1,), (1,)))
        grad = grad + r * (back - (r * mean) * xb_st[s])

    @pl.when(side == 1)
    def _():
        hop_out[1] = grad.astype(BF16)
        hop(1).start()
        for t in others():
            give_d(t).start()

    c_in[slot(here), :] = c_out[pl.ds(here, 1)][0]
    d_in[slot(here), :] = d_out[pl.ds(here, 1)][0]
    for t in others():
        copy_to(c_out.at[t], c_in.at[slot(t)], c_s.at[t], c_r.at[t], device(t)).wait_recv()
        copy_to(d_out.at[t], d_in.at[slot(t)], d_s.at[t], d_r.at[t], device(t)).wait_recv()

    gram[...] = dot(c_in[...].T, d_in[...]).astype(BF16)
    own = width // streams
    b1, b2 = own // RING, own // RING // RING
    hf = b1 // 2
    per = 17

    def rows_at(start, size):
        return pl.ds(pl.multiple_of(start, size), size)

    def along(st, stage, v):
        if st % 2 == stage:
            return at(v, cy, zh)
        return at(cx, v, zh)

    def add(*parts):
        total_ = parts[0].astype(F32)
        for p in parts[1:]:
            total_ += p.astype(F32)
        return total_.astype(BF16)

    def stream(st):
        base = st * own
        pos, pos2 = (cx, cy) if st % 2 == 0 else (cy, cx)
        right, left, opposite = turn(pos, 1), turn(pos, 3), turn(pos, 2)
        n0 = st * per

        def send(k, src, dst, to):
            return copy_to(src, dst, ar_s.at[n0 + k], ar_r.at[n0 + k], to)

        def blk(owner, part_no):
            return rows_at(base + owner * b1 + part_no * hf, hf)

        def over(k, owner, part_no, to):
            return send(k, part.at[blk(owner, part_no)], big_in.at[st, k], along(st, 0, to))

        scat = [
            over(0, opposite, 0, right), over(1, opposite, 1, left), over(2, right, 1, right),
            over(3, left, 0, left), over(4, right, 0, right), over(5, left, 1, left),
        ]

        def sub(v):
            return rows_at(v * b2, b2)

        scat2 = [
            send(5 + o, mid.at[st, sub(turn(pos2, o))], mid_in.at[st, o - 1],
                 along(st, 1, turn(pos2, o)))
            for o in range(1, RING)
        ]
        swap = send(9, mid.at[st, pl.ds(b1, b2)], z_in.at[st], at(cx, cy, 1 - zh))
        mine_sl = rows_at(base + pos * b1 + pos2 * b2, b2)
        gath2 = [
            send(9 + o, res.at[mine_sl], res.at[mine_sl], along(st, 1, turn(pos2, o)))
            for o in range(1, RING)
        ]

        def whole(k, owner, off, n, to):
            sl = rows_at(base + owner * b1 + off, n)
            return send(13 + k, res.at[sl], res.at[sl], along(st, 0, to))

        gath = [
            whole(0, pos, 0, b1, right), whole(1, pos, 0, b1, left),
            whole(2, left, 0, hf, right), whole(3, right, hf, hf, left),
        ]
        store = pltpu.make_async_copy(
            res.at[pl.ds(base, own)], out_hbm.at[pl.ds(base, own)], st_sem.at[st]
        )

        def product():
            sl = pl.ds(base, own)
            part[sl, :] = (dot(emb_t[sl, :], d_in[...]) + dot(basis[sl, :], gram[...])).astype(BF16)
            for k in range(4):
                scat[k].start()

        def pass_right():
            scat[0].wait_recv()
            part[blk(right, 0), :] = add(part[blk(right, 0), :], big_in[st, 0])
            scat[4].start()

        def pass_left():
            scat[1].wait_recv()
            part[blk(left, 1), :] = add(part[blk(left, 1), :], big_in[st, 1])
            scat[5].start()

        def block_done():
            scat[3].wait_recv()
            scat[4].wait_recv()
            mid[st, 0:hf, :] = add(part[blk(pos, 0), :], big_in[st, 3], big_in[st, 4])
            scat[2].wait_recv()
            scat[5].wait_recv()
            mid[st, hf:b1, :] = add(part[blk(pos, 1), :], big_in[st, 2], big_in[st, 5])
            for m in scat2:
                m.start()

        def sub_done():
            for m in scat2:
                m.wait_recv()
            mid[st, b1 : b1 + b2, :] = add(
                mid[st, sub(pos2), :], mid_in[st, 0], mid_in[st, 1], mid_in[st, 2]
            )
            swap.start()

        def total_done():
            swap.wait_recv()
            res[mine_sl, :] = add(mid[st, b1 : b1 + b2, :], z_in[st])
            for m in gath2:
                m.start()

        def block_back():
            for m in gath2:
                m.wait_recv()
            gath[0].start()
            gath[1].start()

        def forward_right():
            gath[0].wait_recv()
            gath[2].start()

        def forward_left():
            gath[1].wait_recv()
            gath[3].start()

        def out():
            gath[2].wait_recv()
            gath[3].wait_recv()
            store.start()

        def finish():
            for m in scat + scat2 + [swap] + gath2 + gath:
                m.wait_send()
            store.wait()

        stages = [
            product, pass_right, pass_left, block_done, sub_done, total_done, block_back,
            forward_right, forward_left, out,
        ]
        return stages, finish

    made = [stream(st) for st in range(streams)]
    order = sorted(
        (times[0][k] + times[1][k] * (st // 2), st, k) for st in range(streams) for k in range(10)
    )
    for _, st, k in order:
        made[st][0][k]()
    for st in range(streams):
        made[st][1]()

    share(1, here, far).wait_send()
    share(0, here, twin).wait_send()
    share(2, far, twin).wait_send()
    for t in others():
        give_e(t).wait_send()
        give_c(t).wait_send()
        give_d(t).wait_send()

    @pl.when(side == 0)
    def _():
        hop(0).wait_send()

    @pl.when(side == 1)
    def _():
        hop(1).wait_send()


def place(src, dst, hold, sem):
    parts = sem.shape[1]
    n = src.shape[0] // parts
    cut = [pl.ds(i * n, n) for i in range(parts)]
    ins = [pltpu.make_async_copy(src.at[c], hold.at[c], sem.at[0, i]) for i, c in enumerate(cut)]
    outs = [pltpu.make_async_copy(hold.at[c], dst.at[c], sem.at[1, i]) for i, c in enumerate(cut)]
    for m in ins:
        m.start()
    for m, o in zip(ins, outs):
        m.wait()
        o.start()
    for o in outs:
        o.wait()


def on_device(byte_ids, patch_len, table, basis, w_down, w_up, dcoef):
    sections = lax.axis_size("section")
    batches, here, _ = byte_ids.shape
    rows = batches * here
    width, rank = basis.shape
    hidden = w_down.shape[2]
    group = sections // 2
    mine = rows // group
    tiles = 8
    streams = STREAMS
    ids = jnp.transpose(byte_ids, (0, 2, 1))
    b1 = width // streams // RING
    b2 = b1 // RING
    vmem = pl.BlockSpec(memory_space=pltpu.VMEM)
    hbm = pl.BlockSpec(memory_space=pl.ANY)
    dma = pltpu.SemaphoreType.DMA
    scratch = [
        pltpu.VMEM((table.shape[0], width), BF16),
        pltpu.VMEM((width, rank), BF16),
        pltpu.VMEM((width, hidden), BF16),
        pltpu.VMEM((width, hidden), BF16),
        pltpu.VMEM((rows, width), BF16),
        pltpu.VMEM((width, rows), BF16),
        pltpu.VMEM((width, hidden), BF16),
        pltpu.VMEM((width, hidden), BF16),
        pltpu.VMEM((3, rank, hidden), F32),
        pltpu.VMEM((rows, hidden), F32),
        pltpu.VMEM((rows, table.shape[0]), BF16),
        pltpu.VMEM((rank, hidden), BF16),
        pltpu.VMEM((group, 2, rank, hidden), BF16),
        pltpu.VMEM((rows, hidden), BF16),
        pltpu.VMEM((group, mine, hidden), BF16),
        pltpu.VMEM((group, mine, hidden), F32),
        pltpu.VMEM((group, mine, rank), F32),
        pltpu.VMEM((group, mine, 1), F32),
        pltpu.VMEM((group, mine, rank), BF16),
        pltpu.VMEM((group, mine, hidden), BF16),
        pltpu.VMEM((rows, rank), BF16),
        pltpu.VMEM((rows, hidden), BF16),
        pltpu.VMEM((rows, 1), F32),
        pltpu.VMEM((2, mine, rank), BF16),
        pltpu.VMEM((2, mine, rank), BF16),
        pltpu.VMEM((streams, 6, b1 // 2, hidden), BF16),
        pltpu.VMEM((streams, b1 + b2, hidden), BF16),
        pltpu.VMEM((streams, 3, b2, hidden), BF16),
        pltpu.VMEM((streams, b2, hidden), BF16),
        dma((4, tiles)), dma((3,)), dma((3,)),
        dma((group,)), dma((group,)), dma((group,)), dma((group,)), dma((group,)), dma((group,)),
        dma((2,)), dma((2,)), dma((streams * 17,)), dma((streams * 17,)), dma((streams,)),
    ]
    out = pl.pallas_call(
        functools.partial(kernel, streams, TIMES[streams]),
        out_shape=jax.ShapeDtypeStruct((width, hidden), BF16),
        in_specs=[vmem, vmem, hbm, hbm, hbm, hbm, hbm],
        out_specs=hbm,
        scratch_shapes=scratch,
        compiler_params=pltpu.CompilerParams(
            collective_id=0, has_side_effects=True, vmem_limit_bytes=56 * 1024 * 1024
        ),
    )(ids, patch_len, table, basis, w_down[0], w_up[0], dcoef.reshape(rows, rank))
    out = pl.pallas_call(
        place,
        out_shape=jax.ShapeDtypeStruct((width, hidden), BF16),
        in_specs=[hbm],
        out_specs=hbm,
        scratch_shapes=[pltpu.VMEM((width, hidden), BF16), dma((2, 4))],
    )(out)
    return out[None]


def solution(mesh):
    return jax.shard_map(
        on_device,
        mesh=mesh,
        in_specs=(
            P(None, "dp", None),
            P(None, "dp"),
            P(),
            P(),
            P("section", None, None),
            P("section", None, None),
            P(None, "dp", None),
        ),
        out_specs=P("section", None, None),
        check_vma=False,
    )
```

```python
import functools

import jax
import jax.numpy as jnp
from jax import lax
from jax.experimental import pallas as pl
from jax.experimental.pallas import tpu as pltpu
from jax.sharding import PartitionSpec as P

MESH = pl.DeviceIdType.MESH
RING = 4
F32, BF16 = jnp.float32, jnp.bfloat16
STREAMS = 4
HALVES = 1
PR = 256
TIMES = {
    4: ((0, 4.2, 4.2, 8.4, 13, 18.5, 23, 28, 28, 32), (1, 2.8, 2.8, 2.8, 2.8, 2.8, 2.8, 2.8, 2.8, 2.8)),
}


def dot(a, b, dims=((1,), (0,))):
    return lax.dot_general(a, b, (dims, ((), ())), preferred_element_type=F32)


def sigmoid(v):
    return 0.5 + 0.5 * jnp.tanh(0.5 * v)


def kernel(
    streams, times,
    ids_ref, len_ref, table_hbm, basis_hbm, down_hbm, up_hbm, dcoef_hbm, out_hbm,
    table, basis, down, up, emb, emb_t, part, res,
    acc_s, acc_e, counts, gram, shared, turned, own_e, all_e,
    z_st, xb_st, r_st, c_out, d_out, c_in, d_in, small, fb_st, e2_st, hop_out, hop_in,
    big_in, mid, mid_in, z_in,
    load_sem, mu_s, mu_r, e_s, e_r, c_s, c_r, d_s, d_r, hop_s, hop_r, ar_s, ar_r, st_sem,
):
    sections = lax.axis_size("section")
    group = all_e.shape[0]
    me = lax.axis_index("section")
    dp = lax.axis_index("dp")
    zh = lax.rem(dp, 2)
    cx = lax.rem(dp // 2, RING)
    cy = dp // (2 * RING)
    width, rank = basis.shape
    rows = emb.shape[0]
    mine = rows // group
    tiles = load_sem.shape[1]
    tile = width // tiles
    side = me // group
    here = lax.rem(me, group)
    partner = lax.rem(me + group, sections)

    def copy_to(src, dst, ssem, rsem, where):
        return pltpu.make_async_remote_copy(
            src_ref=src, dst_ref=dst, send_sem=ssem, recv_sem=rsem,
            device_id=where, device_id_type=MESH,
        )

    def others():
        for off in range(1, group):
            yield lax.rem(here + off, group)

    def device(t):
        return {"section": side * group + t}

    def at(x, y, z):
        return {"dp": (y * RING + x) * 2 + z}

    def turn(v, k):
        return lax.rem(v + k, RING)

    def load(n, i):
        src = (basis_hbm, down_hbm, up_hbm, table_hbm)[n]
        dst = (basis, down, up, table)[n]
        sl = pl.ds(pl.multiple_of(i * tile, tile), tile)
        if n == 3:
            return pltpu.make_async_copy(src.at[:, sl], dst.at[:, sl], load_sem.at[n, i])
        return pltpu.make_async_copy(src.at[sl, :], dst.at[sl, :], load_sem.at[n, i])

    for i in range(tiles):
        for n in range(3):
            load(n, i).start()
    for i in range(tiles):
        load(3, i).start()

    barrier = pltpu.get_barrier_semaphore()
    mates = [device(t) for t in others()] + [{"section": partner}]
    mates += [at(turn(cx, k), cy, zh) for k in range(1, RING)]
    mates += [at(cx, turn(cy, k), zh) for k in range(1, RING)]
    mates += [at(cx, cy, 1 - zh)]
    for mate in mates:
        pl.semaphore_signal(barrier, inc=1, device_id=mate, device_id_type=MESH)

    acc_s[...] = jnp.zeros_like(acc_s)

    @pl.loop(0, tiles)
    def _(i):
        for n in range(3):
            load(n, i).wait()
        sl = pl.ds(pl.multiple_of(i * tile, tile), tile)
        bt = basis[sl, :].T
        acc_s[0] += dot(bt, basis[sl, :])
        acc_s[1] += dot(bt, down[sl, :])
        acc_s[2] += dot(bt, up[sl, :])

    gram[...] = acc_s[0].astype(BF16)
    shared[pl.ds(here, 1), 0] = acc_s[1].astype(BF16)[None]
    shared[pl.ds(here, 1), 1] = acc_s[2].T.astype(BF16)[None]

    pl.semaphore_wait(barrier, len(mates))

    twin = here + 1 - 2 * lax.rem(here, 2)
    far = lax.rem(here + 2, group)
    far_twin = lax.rem(twin + 2, group)

    def share(k, what, to):
        return copy_to(shared.at[what], shared.at[what], mu_s.at[k], mu_r.at[k], device(to))

    share(1, here, far).start()
    share(0, here, twin).start()

    batches, slots, here_rows = ids_ref.shape
    codes = lax.broadcasted_iota(jnp.int32, (table.shape[0], here_rows), 0)
    for m in range(batches):
        total = jnp.zeros(codes.shape, F32)
        for j in range(slots):
            live = jnp.where(len_ref[m : m + 1, :] > j, ids_ref[m, j : j + 1, :], -1)
            total += jnp.where(live == codes, 1.0, 0.0)
        total = total.T
        rs = slice(m * here_rows, (m + 1) * here_rows)
        counts[rs, :] = total.astype(BF16)
        small[rs, :] = lax.rsqrt(jnp.sum(total, axis=1, keepdims=True))
    acc_e[...] = jnp.zeros_like(acc_e)
    step = rows // 4

    @pl.loop(0, tiles)
    def _(i):
        load(3, i).wait()
        sl = pl.ds(pl.multiple_of(i * tile, tile), tile)
        for q in range(2):
            rs = slice(q * rows // 2, (q + 1) * rows // 2)
            pre = dot(counts[rs, :], table[:, sl]) * small[rs, :]
            anchor = (pre * sigmoid(pre)).astype(BF16)
            emb[rs, sl] = anchor
            acc_e[rs, :] += dot(anchor, down[sl, :])

    own_e[...] = acc_e[...].astype(BF16)

    def slot(t):
        return pl.ds(pl.multiple_of(t * mine, mine), mine)

    def give_e(t):
        return copy_to(own_e.at[slot(t)], all_e.at[here], e_s.at[t], e_r.at[here], device(t))

    for t in others():
        give_e(t).start()
    all_e[pl.ds(here, 1)] = own_e[slot(here), :][None]

    fb = jnp.zeros((mine, rank), F32)
    e2 = jnp.zeros((mine, 1), F32)
    for i in range(tiles):
        piece = emb[slot(here), i * tile : (i + 1) * tile]
        fb += dot(piece, basis[i * tile : (i + 1) * tile, :])
        wide = piece.astype(F32)
        e2 += jnp.sum(wide * wide, axis=1, keepdims=True)
    fb_st[...] = fb
    e2_st[...] = e2

    share(1, far, far).wait_recv()
    share(2, far, twin).start()

    def flip():
        @pl.loop(0, group)
        def _(s):
            for n in range(2):
                turned[s, n] = shared[s, n].T

        @pl.loop(0, tiles)
        def _(i):
            sl = pl.ds(pl.multiple_of(i * tile, tile), tile)
            for q in range(4):
                rs = slice(q * step, (q + 1) * step)
                emb_t[sl, rs] = emb[rs, sl].T

    share(0, twin, twin).wait_recv()
    share(2, far_twin, twin).wait_recv()
    for t in others():
        copy_to(own_e.at[slot(t)], all_e.at[t], e_s.at[t], e_r.at[t], device(t)).wait_recv()

    part_rows = mine // HALVES

    def cut(k):
        return pl.ds(k * part_rows, part_rows)

    def sub_slot(t, k):
        return pl.ds(pl.multiple_of(t * mine + k * part_rows, part_rows), part_rows)

    def give(out, into, ssem, rsem, t, k, source):
        return copy_to(
            out.at[t, cut(k)], into.at[sub_slot(source, k)], ssem.at[t, k], rsem.at[source, k],
            device(t),
        )

    def give_c(t, k):
        return give(c_out, c_in, c_s, c_r, t, k, here)

    def give_d(t, k):
        return give(d_out, d_in, d_s, d_r, t, k, here)

    def hop(n, k):
        return copy_to(
            hop_out.at[n, cut(k)], hop_in.at[n, cut(k)], hop_s.at[n, k], hop_r.at[n, k],
            {"section": partner},
        )

    inv = 1.0 / width

    def up_part(k, coef):
        fb, e2 = fb_st[cut(k), :], e2_st[cut(k), :]

        def step_up(s, coef):
            cb = coef.astype(BF16)
            c_out[s, cut(k)] = cb
            cg = dot(cb, gram[...])
            xb = fb + cg
            sq = e2 + jnp.sum(coef * (fb + xb), axis=1, keepdims=True)
            r = lax.rsqrt(jnp.maximum(sq, 0.0) * inv + 1e-06)
            z = r * (all_e[s, cut(k)].astype(F32) + dot(cb, shared[s, 0]))
            z_st[s, cut(k)] = z
            xb_st[s, cut(k)] = xb
            r_st[s, cut(k)] = r
            act = (z * sigmoid(z)).astype(BF16)
            return coef + dot(act, shared[s, 1])

        return lax.fori_loop(0, group, step_up, coef, unroll=True)

    def down_part(k, grad, then):
        def step_down(i, grad):
            s = group - 1 - i
            da = dot(grad.astype(BF16), turned[s, 1])
            z = z_st[s, cut(k)]
            r = r_st[s, cut(k)]
            sig = sigmoid(z)
            dz = da * sig * (1.0 + z * (1.0 - sig))
            d_out[s, cut(k)] = (r * dz).astype(BF16)
            then(s)
            mean = jnp.sum(dz * z, axis=1, keepdims=True) * inv
            back = dot(dz.astype(BF16), turned[s, 0])
            return grad + r * (back - (r * mean) * xb_st[s, cut(k)])

        return lax.fori_loop(0, group, step_down, grad, unroll=True)

    @pl.when(side == 0)
    def _():
        for k in range(HALVES):
            coef = up_part(k, jnp.zeros((part_rows, rank), F32))
            hop_out[0, cut(k)] = coef.astype(BF16)
            hop(0, k).start()
        for t in others():
            for k in range(HALVES):
                give_c(t, k).start()
        flip()
        for k in range(HALVES):
            hop(1, k).wait_recv()

            def send_on(s):
                @pl.when(here != s)
                def _():
                    give_d(s, k).start()

            down_part(k, hop_in[1, cut(k)].astype(F32), send_on)

    @pl.when(side == 1)
    def _():
        last = pltpu.make_async_copy(dcoef_hbm.at[slot(here)], hop_in.at[1], st_sem.at[0])
        last.start()
        flip()
        last.wait()
        for k in range(HALVES):
            hop(0, k).wait_recv()
            up_part(k, hop_in[0, cut(k)].astype(F32))
            grad = down_part(k, hop_in[1, cut(k)].astype(F32), lambda s: None)
            hop_out[1, cut(k)] = grad.astype(BF16)
            hop(1, k).start()
        for t in others():
            for k in range(HALVES):
                give_c(t, k).start()
                give_d(t, k).start()

    c_in[slot(here), :] = c_out[pl.ds(here, 1)][0]
    d_in[slot(here), :] = d_out[pl.ds(here, 1)][0]
    for t in others():
        for k in range(HALVES):
            give(c_out, c_in, c_s, c_r, t, k, t).wait_recv()
            give(d_out, d_in, d_s, d_r, t, k, t).wait_recv()

    def clean():
        share(1, here, far).wait_send()
        share(0, here, twin).wait_send()
        share(2, far, twin).wait_send()
        for t in others():
            give_e(t).wait_send()
            for k in range(HALVES):
                give_c(t, k).wait_send()
                give_d(t, k).wait_send()

        @pl.when(side == 0)
        def _():
            for k in range(HALVES):
                hop(0, k).wait_send()

        @pl.when(side == 1)
        def _():
            for k in range(HALVES):
                hop(1, k).wait_send()

    gram[...] = dot(c_in[...].T, d_in[...]).astype(BF16)
    own = width // streams
    b1, b2 = own // RING, own // RING // RING
    hf = b1 // 2
    per = 17

    def rows_at(start, size):
        return pl.ds(pl.multiple_of(start, size), size)

    def along(st, stage, v):
        if st % 2 == stage:
            return at(v, cy, zh)
        return at(cx, v, zh)

    def add(*parts):
        total_ = parts[0].astype(F32)
        for p in parts[1:]:
            total_ += p.astype(F32)
        return total_.astype(BF16)

    def stream(st):
        base = st * own
        pos, pos2 = (cx, cy) if st % 2 == 0 else (cy, cx)
        right, left, opposite = turn(pos, 1), turn(pos, 3), turn(pos, 2)
        n0 = st * per

        def send(k, src, dst, to):
            return copy_to(src, dst, ar_s.at[n0 + k], ar_r.at[n0 + k], to)

        def blk(owner, part_no):
            return rows_at(base + owner * b1 + part_no * hf, hf)

        def over(k, owner, part_no, to):
            return send(k, part.at[blk(owner, part_no)], big_in.at[st, k], along(st, 0, to))

        scat = [
            over(0, opposite, 0, right), over(1, opposite, 1, left), over(2, right, 1, right),
            over(3, left, 0, left), over(4, right, 0, right), over(5, left, 1, left),
        ]

        def sub(v):
            return rows_at(v * b2, b2)

        scat2 = [
            send(5 + o, mid.at[st, sub(turn(pos2, o))], mid_in.at[st, o - 1],
                 along(st, 1, turn(pos2, o)))
            for o in range(1, RING)
        ]
        swap = send(9, mid.at[st, pl.ds(b1, b2)], z_in.at[st], at(cx, cy, 1 - zh))
        mine_sl = rows_at(base + pos * b1 + pos2 * b2, b2)
        gath2 = [
            send(9 + o, res.at[mine_sl], res.at[mine_sl], along(st, 1, turn(pos2, o)))
            for o in range(1, RING)
        ]

        def whole(k, owner, off, n, to):
            sl = rows_at(base + owner * b1 + off, n)
            return send(13 + k, res.at[sl], res.at[sl], along(st, 0, to))

        gath = [
            whole(0, pos, 0, b1, right), whole(1, pos, 0, b1, left),
            whole(2, left, 0, hf, right), whole(3, right, hf, hf, left),
        ]
        store = pltpu.make_async_copy(
            res.at[pl.ds(base, own)], out_hbm.at[pl.ds(base, own)], st_sem.at[st]
        )

        def product():
            @pl.loop(0, own // PR)
            def _(i):
                sl = rows_at(base + i * PR, PR)
                value = dot(emb_t[sl, :], d_in[...]) + dot(basis[sl, :], gram[...])
                part[sl, :] = value.astype(BF16)

            for k in range(4):
                scat[k].start()

        def pass_right():
            scat[0].wait_recv()
            part[blk(right, 0), :] = add(part[blk(right, 0), :], big_in[st, 0])
            scat[4].start()

        def pass_left():
            scat[1].wait_recv()
            part[blk(left, 1), :] = add(part[blk(left, 1), :], big_in[st, 1])
            scat[5].start()

        def block_done():
            scat[3].wait_recv()
            scat[4].wait_recv()
            mid[st, 0:hf, :] = add(part[blk(pos, 0), :], big_in[st, 3], big_in[st, 4])
            scat[2].wait_recv()
            scat[5].wait_recv()
            mid[st, hf:b1, :] = add(part[blk(pos, 1), :], big_in[st, 2], big_in[st, 5])
            for m in scat2:
                m.start()

        def sub_done():
            for m in scat2:
                m.wait_recv()
            mid[st, b1 : b1 + b2, :] = add(
                mid[st, sub(pos2), :], mid_in[st, 0], mid_in[st, 1], mid_in[st, 2]
            )
            swap.start()
            for m in scat:
                m.wait_send()

        def total_done():
            swap.wait_recv()
            res[mine_sl, :] = add(mid[st, b1 : b1 + b2, :], z_in[st])
            for m in gath2:
                m.start()

        def block_back():
            for m in gath2:
                m.wait_recv()
            gath[0].start()
            gath[1].start()
            for m in scat2 + [swap] + gath2:
                m.wait_send()

        def forward_right():
            gath[0].wait_recv()
            gath[2].start()

        def forward_left():
            gath[1].wait_recv()
            gath[3].start()

        def out():
            gath[2].wait_recv()
            gath[3].wait_recv()
            store.start()

        def finish():
            for m in gath:
                m.wait_send()
            store.wait()

        stages = [
            product, pass_right, pass_left, block_done, sub_done, total_done, block_back,
            forward_right, forward_left, out,
        ]
        return stages, finish

    made = [stream(st) for st in range(streams)]
    order = sorted(
        (times[0][k] + times[1][k] * (st // 2), st, k) for st in range(streams) for k in range(10)
    )
    for n, (_, st, k) in enumerate(order):
        if n == streams:
            clean()
        made[st][0][k]()
    for st in range(streams):
        made[st][1]()


def place(src, dst, hold, sem):
    parts = sem.shape[1]
    n = src.shape[0] // parts
    cut = [pl.ds(i * n, n) for i in range(parts)]
    ins = [pltpu.make_async_copy(src.at[c], hold.at[c], sem.at[0, i]) for i, c in enumerate(cut)]
    outs = [pltpu.make_async_copy(hold.at[c], dst.at[c], sem.at[1, i]) for i, c in enumerate(cut)]
    for m in ins:
        m.start()
    for m, o in zip(ins, outs):
        m.wait()
        o.start()
    for o in outs:
        o.wait()


def on_device(byte_ids, patch_len, table, basis, w_down, w_up, dcoef):
    sections = lax.axis_size("section")
    batches, here, _ = byte_ids.shape
    rows = batches * here
    width, rank = basis.shape
    hidden = w_down.shape[2]
    group = sections // 2
    mine = rows // group
    tiles = 8
    streams = STREAMS
    ids = jnp.transpose(byte_ids, (0, 2, 1))
    b1 = width // streams // RING
    b2 = b1 // RING
    vmem = pl.BlockSpec(memory_space=pltpu.VMEM)
    hbm = pl.BlockSpec(memory_space=pl.ANY)
    dma = pltpu.SemaphoreType.DMA
    scratch = [
        pltpu.VMEM((table.shape[0], width), BF16),
        pltpu.VMEM((width, rank), BF16),
        pltpu.VMEM((width, hidden), BF16),
        pltpu.VMEM((width, hidden), BF16),
        pltpu.VMEM((rows, width), BF16),
        pltpu.VMEM((width, rows), BF16),
        pltpu.VMEM((width, hidden), BF16),
        pltpu.VMEM((width, hidden), BF16),
        pltpu.VMEM((3, rank, hidden), F32),
        pltpu.VMEM((rows, hidden), F32),
        pltpu.VMEM((rows, table.shape[0]), BF16),
        pltpu.VMEM((rank, hidden), BF16),
        pltpu.VMEM((group, 2, rank, hidden), BF16),
        pltpu.VMEM((group, 2, hidden, rank), BF16),
        pltpu.VMEM((rows, hidden), BF16),
        pltpu.VMEM((group, mine, hidden), BF16),
        pltpu.VMEM((group, mine, hidden), F32),
        pltpu.VMEM((group, mine, rank), F32),
        pltpu.VMEM((group, mine, 1), F32),
        pltpu.VMEM((group, mine, rank), BF16),
        pltpu.VMEM((group, mine, hidden), BF16),
        pltpu.VMEM((rows, rank), BF16),
        pltpu.VMEM((rows, hidden), BF16),
        pltpu.VMEM((rows, 1), F32),
        pltpu.VMEM((mine, rank), F32),
        pltpu.VMEM((mine, 1), F32),
        pltpu.VMEM((2, mine, rank), BF16),
        pltpu.VMEM((2, mine, rank), BF16),
        pltpu.VMEM((streams, 6, b1 // 2, hidden), BF16),
        pltpu.VMEM((streams, b1 + b2, hidden), BF16),
        pltpu.VMEM((streams, 3, b2, hidden), BF16),
        pltpu.VMEM((streams, b2, hidden), BF16),
        dma((4, tiles)), dma((3,)), dma((3,)),
        dma((group,)), dma((group,)), dma((group, HALVES)), dma((group, HALVES)),
        dma((group, HALVES)), dma((group, HALVES)), dma((2, HALVES)), dma((2, HALVES)), dma((streams * 17,)), dma((streams * 17,)), dma((streams,)),
    ]
    out = pl.pallas_call(
        functools.partial(kernel, streams, TIMES[streams]),
        out_shape=jax.ShapeDtypeStruct((width, hidden), BF16),
        in_specs=[vmem, vmem, hbm, hbm, hbm, hbm, hbm],
        out_specs=hbm,
        scratch_shapes=scratch,
        compiler_params=pltpu.CompilerParams(
            collective_id=0, has_side_effects=True, vmem_limit_bytes=56 * 1024 * 1024
        ),
    )(ids, patch_len, table, basis, w_down[0], w_up[0], dcoef.reshape(rows, rank))
    out = pl.pallas_call(
        place,
        out_shape=jax.ShapeDtypeStruct((width, hidden), BF16),
        in_specs=[hbm],
        out_specs=hbm,
        scratch_shapes=[pltpu.VMEM((width, hidden), BF16), dma((2, 4))],
    )(out)
    return out[None]


def solution(mesh):
    return jax.shard_map(
        on_device,
        mesh=mesh,
        in_specs=(
            P(None, "dp", None),
            P(None, "dp"),
            P(),
            P(),
            P("section", None, None),
            P("section", None, None),
            P(None, "dp", None),
        ),
        out_specs=P("section", None, None),
        check_vma=False,
    )
```

```python
import functools

import jax
import jax.numpy as jnp
from jax import lax
from jax.experimental import pallas as pl
from jax.experimental.pallas import tpu as pltpu
from jax.sharding import PartitionSpec as P

MESH = pl.DeviceIdType.MESH
RING = 4
F32, BF16 = jnp.float32, jnp.bfloat16
STREAMS = 4
HALVES = 1
PR = 256
TIMES = {
    4: ((0, 4.2, 4.2, 8.4, 13, 18.5, 23, 28, 28, 32), (1, 2.8, 2.8, 2.8, 2.8, 2.8, 2.8, 2.8, 2.8, 2.8)),
}


def dot(a, b, dims=((1,), (0,))):
    return lax.dot_general(a, b, (dims, ((), ())), preferred_element_type=F32)


def sigmoid(v):
    return 0.5 + 0.5 * jnp.tanh(0.5 * v)


def kernel(
    streams, times,
    ids_ref, len_ref, table_hbm, basis_hbm, down_hbm, up_hbm, dcoef_hbm, out_hbm,
    table, basis, down, up, emb, emb_t, part, res,
    acc_s, acc_e, counts, gram, shared, turned, chain, own_e, all_e,
    z_st, xb_st, r_st, c_out, d_out, c_in, d_in, small, fb_st, e2_st, hop_out, hop_in,
    big_in, mid, mid_in, z_in,
    load_sem, mu_s, mu_r, e_s, e_r, c_s, c_r, d_s, d_r, hop_s, hop_r, ar_s, ar_r, st_sem,
):
    sections = lax.axis_size("section")
    group = all_e.shape[0]
    me = lax.axis_index("section")
    dp = lax.axis_index("dp")
    zh = lax.rem(dp, 2)
    cx = lax.rem(dp // 2, RING)
    cy = dp // (2 * RING)
    width, rank = basis.shape
    rows = emb.shape[0]
    mine = rows // group
    tiles = load_sem.shape[1]
    tile = width // tiles
    side = me // group
    here = lax.rem(me, group)
    partner = lax.rem(me + group, sections)

    def copy_to(src, dst, ssem, rsem, where):
        return pltpu.make_async_remote_copy(
            src_ref=src, dst_ref=dst, send_sem=ssem, recv_sem=rsem,
            device_id=where, device_id_type=MESH,
        )

    def others():
        for off in range(1, group):
            yield lax.rem(here + off, group)

    def device(t):
        return {"section": side * group + t}

    def at(x, y, z):
        return {"dp": (y * RING + x) * 2 + z}

    def turn(v, k):
        return lax.rem(v + k, RING)

    def load(n, i):
        src = (basis_hbm, down_hbm, up_hbm, table_hbm)[n]
        dst = (basis, down, up, table)[n]
        sl = pl.ds(pl.multiple_of(i * tile, tile), tile)
        if n == 3:
            return pltpu.make_async_copy(src.at[:, sl], dst.at[:, sl], load_sem.at[n, i])
        return pltpu.make_async_copy(src.at[sl, :], dst.at[sl, :], load_sem.at[n, i])

    for i in range(tiles):
        for n in range(3):
            load(n, i).start()
    for i in range(tiles):
        load(3, i).start()

    barrier = pltpu.get_barrier_semaphore()
    mates = [device(t) for t in others()] + [{"section": partner}]
    mates += [at(turn(cx, k), cy, zh) for k in range(1, RING)]
    mates += [at(cx, turn(cy, k), zh) for k in range(1, RING)]
    mates += [at(cx, cy, 1 - zh)]
    for mate in mates:
        pl.semaphore_signal(barrier, inc=1, device_id=mate, device_id_type=MESH)

    acc_s[...] = jnp.zeros_like(acc_s)

    @pl.loop(0, tiles)
    def _(i):
        for n in range(3):
            load(n, i).wait()
        sl = pl.ds(pl.multiple_of(i * tile, tile), tile)
        bt = basis[sl, :].T
        acc_s[0] += dot(bt, basis[sl, :])
        acc_s[1] += dot(bt, down[sl, :])
        acc_s[2] += dot(bt, up[sl, :])

    gram[...] = acc_s[0].astype(BF16)
    shared[pl.ds(here, 1), 0] = acc_s[1].astype(BF16)[None]
    shared[pl.ds(here, 1), 1] = acc_s[2].T.astype(BF16)[None]

    pl.semaphore_wait(barrier, len(mates))

    twin = here + 1 - 2 * lax.rem(here, 2)
    far = lax.rem(here + 2, group)
    far_twin = lax.rem(twin + 2, group)

    def share(k, what, to):
        return copy_to(shared.at[what], shared.at[what], mu_s.at[k], mu_r.at[k], device(to))

    share(1, here, far).start()
    share(0, here, twin).start()

    batches, slots, here_rows = ids_ref.shape
    codes = lax.broadcasted_iota(jnp.int32, (table.shape[0], here_rows), 0)
    for m in range(batches):
        total = jnp.zeros(codes.shape, F32)
        for j in range(slots):
            live = jnp.where(len_ref[m : m + 1, :] > j, ids_ref[m, j : j + 1, :], -1)
            total += jnp.where(live == codes, 1.0, 0.0)
        total = total.T
        rs = slice(m * here_rows, (m + 1) * here_rows)
        counts[rs, :] = total.astype(BF16)
        small[rs, :] = lax.rsqrt(jnp.sum(total, axis=1, keepdims=True))
    acc_e[...] = jnp.zeros_like(acc_e)
    step = rows // 4

    @pl.loop(0, tiles)
    def _(i):
        load(3, i).wait()
        sl = pl.ds(pl.multiple_of(i * tile, tile), tile)
        for q in range(2):
            rs = slice(q * rows // 2, (q + 1) * rows // 2)
            pre = dot(counts[rs, :], table[:, sl]) * small[rs, :]
            anchor = (pre * sigmoid(pre)).astype(BF16)
            emb[rs, sl] = anchor
            acc_e[rs, :] += dot(anchor, down[sl, :])

    own_e[...] = acc_e[...].astype(BF16)

    def slot(t):
        return pl.ds(pl.multiple_of(t * mine, mine), mine)

    def give_e(t):
        return copy_to(own_e.at[slot(t)], all_e.at[here], e_s.at[t], e_r.at[here], device(t))

    for t in others():
        give_e(t).start()
    all_e[pl.ds(here, 1)] = own_e[slot(here), :][None]

    fb = jnp.zeros((mine, rank), F32)
    e2 = jnp.zeros((mine, 1), F32)
    for i in range(tiles):
        piece = emb[slot(here), i * tile : (i + 1) * tile]
        fb += dot(piece, basis[i * tile : (i + 1) * tile, :])
        wide = piece.astype(F32)
        e2 += jnp.sum(wide * wide, axis=1, keepdims=True)
    fb_st[...] = fb
    e2_st[...] = e2

    share(1, far, far).wait_recv()
    share(2, far, twin).start()

    def flip():
        @pl.loop(0, group)
        def _(s):
            for n in range(2):
                turned[s, n] = shared[s, n].T
            for s in range(group - 1):
                chain[s, 2] = dot(turned[s + 1, 0], turned[s, 1]).astype(BF16)

        @pl.loop(0, tiles)
        def _(i):
            sl = pl.ds(pl.multiple_of(i * tile, tile), tile)
            for q in range(4):
                rs = slice(q * step, (q + 1) * step)
                emb_t[sl, rs] = emb[rs, sl].T

    share(0, twin, twin).wait_recv()
    share(2, far_twin, twin).wait_recv()
    for s in range(group - 1):
        chain[s, 0] = dot(shared[s, 1], shared[s + 1, 0]).astype(BF16)
        chain[s, 1] = dot(shared[s, 1], gram[...]).astype(BF16)
    for t in others():
        copy_to(own_e.at[slot(t)], all_e.at[t], e_s.at[t], e_r.at[t], device(t)).wait_recv()

    part_rows = mine // HALVES

    def cut(k):
        return pl.ds(k * part_rows, part_rows)

    def sub_slot(t, k):
        return pl.ds(pl.multiple_of(t * mine + k * part_rows, part_rows), part_rows)

    def give(out, into, ssem, rsem, t, k, source):
        return copy_to(
            out.at[t, cut(k)], into.at[sub_slot(source, k)], ssem.at[t, k], rsem.at[source, k],
            device(t),
        )

    def give_c(t, k):
        return give(c_out, c_in, c_s, c_r, t, k, here)

    def give_d(t, k):
        return give(d_out, d_in, d_s, d_r, t, k, here)

    def hop(n, k):
        return copy_to(
            hop_out.at[n, cut(k)], hop_in.at[n, cut(k)], hop_s.at[n, k], hop_r.at[n, k],
            {"section": partner},
        )

    inv = 1.0 / width

    def up_part(k, coef):
        fb, e2 = fb_st[cut(k), :], e2_st[cut(k), :]

        cg = cm = None
        for s in range(group):
            cb = coef.astype(BF16)
            c_out[s, cut(k)] = cb
            if s == 0:
                cg = dot(cb, gram[...])
                cm = dot(cb, shared[0, 0])
            xb = fb + cg
            sq = e2 + jnp.sum(coef * (fb + xb), axis=1, keepdims=True)
            r = lax.rsqrt(jnp.maximum(sq, 0.0) * inv + 1e-06)
            z = r * (all_e[s, cut(k)].astype(F32) + cm)
            z_st[s, cut(k)] = z
            xb_st[s, cut(k)] = xb
            r_st[s, cut(k)] = r
            act = (z * sigmoid(z)).astype(BF16)
            if s < group - 1:
                cm = dot(cb, shared[s + 1, 0]) + dot(act, chain[s, 0])
                cg = cg + dot(act, chain[s, 1])
            coef = coef + dot(act, shared[s, 1])
        return coef

    def down_part(k, grad, then):
        da = dot(grad.astype(BF16), turned[group - 1, 1])
        for s in reversed(range(group)):
            z = z_st[s, cut(k)]
            r = r_st[s, cut(k)]
            sig = sigmoid(z)
            dz = da * (sig * (1.0 + z * (1.0 - sig)))
            d_out[s, cut(k)] = (r * dz).astype(BF16)
            then(s)
            dzb = dz.astype(BF16)
            mean = jnp.sum(dz * z, axis=1, keepdims=True) * inv
            if s > 0:
                da = dot(grad.astype(BF16), turned[s - 1, 1]) + r * (
                    dot(dzb, chain[s - 1, 2])
                    - (r * mean) * dot(xb_st[s, cut(k)].astype(BF16), turned[s - 1, 1])
                )
            grad = grad + r * (dot(dzb, turned[s, 0]) - (r * mean) * xb_st[s, cut(k)])
        return grad

    @pl.when(side == 0)
    def _():
        for k in range(HALVES):
            coef = up_part(k, jnp.zeros((part_rows, rank), F32))
            hop_out[0, cut(k)] = coef.astype(BF16)
            hop(0, k).start()
        for t in others():
            for k in range(HALVES):
                give_c(t, k).start()
        flip()
        for k in range(HALVES):
            hop(1, k).wait_recv()

            def send_on(s):
                @pl.when(here != s)
                def _():
                    give_d(s, k).start()

            down_part(k, hop_in[1, cut(k)].astype(F32), send_on)

    @pl.when(side == 1)
    def _():
        last = pltpu.make_async_copy(dcoef_hbm.at[slot(here)], hop_in.at[1], st_sem.at[0])
        last.start()
        flip()
        last.wait()
        for k in range(HALVES):
            hop(0, k).wait_recv()
            up_part(k, hop_in[0, cut(k)].astype(F32))
            grad = down_part(k, hop_in[1, cut(k)].astype(F32), lambda s: None)
            hop_out[1, cut(k)] = grad.astype(BF16)
            hop(1, k).start()
        for t in others():
            for k in range(HALVES):
                give_c(t, k).start()
                give_d(t, k).start()

    c_in[slot(here), :] = c_out[pl.ds(here, 1)][0]
    d_in[slot(here), :] = d_out[pl.ds(here, 1)][0]
    for t in others():
        for k in range(HALVES):
            give(c_out, c_in, c_s, c_r, t, k, t).wait_recv()
            give(d_out, d_in, d_s, d_r, t, k, t).wait_recv()

    def clean():
        share(1, here, far).wait_send()
        share(0, here, twin).wait_send()
        share(2, far, twin).wait_send()
        for t in others():
            give_e(t).wait_send()
            for k in range(HALVES):
                give_c(t, k).wait_send()
                give_d(t, k).wait_send()

        @pl.when(side == 0)
        def _():
            for k in range(HALVES):
                hop(0, k).wait_send()

        @pl.when(side == 1)
        def _():
            for k in range(HALVES):
                hop(1, k).wait_send()

    gram[...] = dot(c_in[...].T, d_in[...]).astype(BF16)
    own = width // streams
    b1, b2 = own // RING, own // RING // RING
    hf = b1 // 2
    per = 17

    def rows_at(start, size):
        return pl.ds(pl.multiple_of(start, size), size)

    def along(st, stage, v):
        if st % 2 == stage:
            return at(v, cy, zh)
        return at(cx, v, zh)

    def add(*parts):
        total_ = parts[0].astype(F32)
        for p in parts[1:]:
            total_ += p.astype(F32)
        return total_.astype(BF16)

    def stream(st):
        base = st * own
        pos, pos2 = (cx, cy) if st % 2 == 0 else (cy, cx)
        right, left, opposite = turn(pos, 1), turn(pos, 3), turn(pos, 2)
        n0 = st * per

        def send(k, src, dst, to):
            return copy_to(src, dst, ar_s.at[n0 + k], ar_r.at[n0 + k], to)

        def blk(owner, part_no):
            return rows_at(base + owner * b1 + part_no * hf, hf)

        def over(k, owner, part_no, to):
            return send(k, part.at[blk(owner, part_no)], big_in.at[st, k], along(st, 0, to))

        scat = [
            over(0, opposite, 0, right), over(1, opposite, 1, left), over(2, right, 1, right),
            over(3, left, 0, left), over(4, right, 0, right), over(5, left, 1, left),
        ]

        def sub(v):
            return rows_at(v * b2, b2)

        scat2 = [
            send(5 + o, mid.at[st, sub(turn(pos2, o))], mid_in.at[st, o - 1],
                 along(st, 1, turn(pos2, o)))
            for o in range(1, RING)
        ]
        swap = send(9, mid.at[st, pl.ds(b1, b2)], z_in.at[st], at(cx, cy, 1 - zh))
        mine_sl = rows_at(base + pos * b1 + pos2 * b2, b2)
        gath2 = [
            send(9 + o, res.at[mine_sl], res.at[mine_sl], along(st, 1, turn(pos2, o)))
            for o in range(1, RING)
        ]

        def whole(k, owner, off, n, to):
            sl = rows_at(base + owner * b1 + off, n)
            return send(13 + k, res.at[sl], res.at[sl], along(st, 0, to))

        gath = [
            whole(0, pos, 0, b1, right), whole(1, pos, 0, b1, left),
            whole(2, left, 0, hf, right), whole(3, right, hf, hf, left),
        ]
        store = pltpu.make_async_copy(
            res.at[pl.ds(base, own)], out_hbm.at[pl.ds(base, own)], st_sem.at[st]
        )

        def product():
            @pl.loop(0, own // PR)
            def _(i):
                sl = rows_at(base + i * PR, PR)
                value = dot(emb_t[sl, :], d_in[...]) + dot(basis[sl, :], gram[...])
                part[sl, :] = value.astype(BF16)

            for k in range(4):
                scat[k].start()

        def pass_right():
            scat[0].wait_recv()
            part[blk(right, 0), :] = add(part[blk(right, 0), :], big_in[st, 0])
            scat[4].start()

        def pass_left():
            scat[1].wait_recv()
            part[blk(left, 1), :] = add(part[blk(left, 1), :], big_in[st, 1])
            scat[5].start()

        def block_done():
            scat[3].wait_recv()
            scat[4].wait_recv()
            mid[st, 0:hf, :] = add(part[blk(pos, 0), :], big_in[st, 3], big_in[st, 4])
            scat[2].wait_recv()
            scat[5].wait_recv()
            mid[st, hf:b1, :] = add(part[blk(pos, 1), :], big_in[st, 2], big_in[st, 5])
            for m in scat2:
                m.start()

        def sub_done():
            for m in scat2:
                m.wait_recv()
            mid[st, b1 : b1 + b2, :] = add(
                mid[st, sub(pos2), :], mid_in[st, 0], mid_in[st, 1], mid_in[st, 2]
            )
            swap.start()
            for m in scat:
                m.wait_send()

        def total_done():
            swap.wait_recv()
            res[mine_sl, :] = add(mid[st, b1 : b1 + b2, :], z_in[st])
            for m in gath2:
                m.start()

        def block_back():
            for m in gath2:
                m.wait_recv()
            gath[0].start()
            gath[1].start()
            for m in scat2 + [swap] + gath2:
                m.wait_send()

        def forward_right():
            gath[0].wait_recv()
            gath[2].start()

        def forward_left():
            gath[1].wait_recv()
            gath[3].start()

        def out():
            gath[2].wait_recv()
            gath[3].wait_recv()
            store.start()

        def finish():
            for m in gath:
                m.wait_send()
            store.wait()

        stages = [
            product, pass_right, pass_left, block_done, sub_done, total_done, block_back,
            forward_right, forward_left, out,
        ]
        return stages, finish

    made = [stream(st) for st in range(streams)]
    order = sorted(
        (times[0][k] + times[1][k] * (st // 2), st, k) for st in range(streams) for k in range(10)
    )
    for n, (_, st, k) in enumerate(order):
        if n == streams:
            clean()
        made[st][0][k]()
    for st in range(streams):
        made[st][1]()


def place(src, dst, hold, sem):
    parts = sem.shape[1]
    n = src.shape[0] // parts
    cut = [pl.ds(i * n, n) for i in range(parts)]
    ins = [pltpu.make_async_copy(src.at[c], hold.at[c], sem.at[0, i]) for i, c in enumerate(cut)]
    outs = [pltpu.make_async_copy(hold.at[c], dst.at[c], sem.at[1, i]) for i, c in enumerate(cut)]
    for m in ins:
        m.start()
    for m, o in zip(ins, outs):
        m.wait()
        o.start()
    for o in outs:
        o.wait()


def on_device(byte_ids, patch_len, table, basis, w_down, w_up, dcoef):
    sections = lax.axis_size("section")
    batches, here, _ = byte_ids.shape
    rows = batches * here
    width, rank = basis.shape
    hidden = w_down.shape[2]
    group = sections // 2
    mine = rows // group
    tiles = 8
    streams = STREAMS
    ids = jnp.transpose(byte_ids, (0, 2, 1))
    b1 = width // streams // RING
    b2 = b1 // RING
    vmem = pl.BlockSpec(memory_space=pltpu.VMEM)
    hbm = pl.BlockSpec(memory_space=pl.ANY)
    dma = pltpu.SemaphoreType.DMA
    scratch = [
        pltpu.VMEM((table.shape[0], width), BF16),
        pltpu.VMEM((width, rank), BF16),
        pltpu.VMEM((width, hidden), BF16),
        pltpu.VMEM((width, hidden), BF16),
        pltpu.VMEM((rows, width), BF16),
        pltpu.VMEM((width, rows), BF16),
        pltpu.VMEM((width, hidden), BF16),
        pltpu.VMEM((width, hidden), BF16),
        pltpu.VMEM((3, rank, hidden), F32),
        pltpu.VMEM((rows, hidden), F32),
        pltpu.VMEM((rows, table.shape[0]), BF16),
        pltpu.VMEM((rank, hidden), BF16),
        pltpu.VMEM((group, 2, rank, hidden), BF16),
        pltpu.VMEM((group, 2, hidden, rank), BF16),
        pltpu.VMEM((group - 1, 3, hidden, hidden), BF16),
        pltpu.VMEM((rows, hidden), BF16),
        pltpu.VMEM((group, mine, hidden), BF16),
        pltpu.VMEM((group, mine, hidden), F32),
        pltpu.VMEM((group, mine, rank), F32),
        pltpu.VMEM((group, mine, 1), F32),
        pltpu.VMEM((group, mine, rank), BF16),
        pltpu.VMEM((group, mine, hidden), BF16),
        pltpu.VMEM((rows, rank), BF16),
        pltpu.VMEM((rows, hidden), BF16),
        pltpu.VMEM((rows, 1), F32),
        pltpu.VMEM((mine, rank), F32),
        pltpu.VMEM((mine, 1), F32),
        pltpu.VMEM((2, mine, rank), BF16),
        pltpu.VMEM((2, mine, rank), BF16),
        pltpu.VMEM((streams, 6, b1 // 2, hidden), BF16),
        pltpu.VMEM((streams, b1 + b2, hidden), BF16),
        pltpu.VMEM((streams, 3, b2, hidden), BF16),
        pltpu.VMEM((streams, b2, hidden), BF16),
        dma((4, tiles)), dma((3,)), dma((3,)),
        dma((group,)), dma((group,)), dma((group, HALVES)), dma((group, HALVES)),
        dma((group, HALVES)), dma((group, HALVES)), dma((2, HALVES)), dma((2, HALVES)), dma((streams * 17,)), dma((streams * 17,)), dma((streams,)),
    ]
    out = pl.pallas_call(
        functools.partial(kernel, streams, TIMES[streams]),
        out_shape=jax.ShapeDtypeStruct((width, hidden), BF16),
        in_specs=[vmem, vmem, hbm, hbm, hbm, hbm, hbm],
        out_specs=hbm,
        scratch_shapes=scratch,
        compiler_params=pltpu.CompilerParams(
            collective_id=0, has_side_effects=True, vmem_limit_bytes=56 * 1024 * 1024
        ),
    )(ids, patch_len, table, basis, w_down[0], w_up[0], dcoef.reshape(rows, rank))
    out = pl.pallas_call(
        place,
        out_shape=jax.ShapeDtypeStruct((width, hidden), BF16),
        in_specs=[hbm],
        out_specs=hbm,
        scratch_shapes=[pltpu.VMEM((width, hidden), BF16), dma((2, 4))],
    )(out)
    return out[None]


def solution(mesh):
    return jax.shard_map(
        on_device,
        mesh=mesh,
        in_specs=(
            P(None, "dp", None),
            P(None, "dp"),
            P(),
            P(),
            P("section", None, None),
            P("section", None, None),
            P(None, "dp", None),
        ),
        out_specs=P("section", None, None),
        check_vma=False,
    )
```

```python
import functools

import jax
import jax.numpy as jnp
from jax import lax
from jax.experimental import pallas as pl
from jax.experimental.pallas import tpu as pltpu
from jax.sharding import PartitionSpec as P

MESH = pl.DeviceIdType.MESH
RING = 4
F32, BF16 = jnp.float32, jnp.bfloat16
HALVES = 1
PR = 256
SIZES = (512,) * 8
ORDER = (
    (0, 0), (1, 0), (2, 0), (3, 0), (4, 0), (5, 0), (6, 0), (7, 0), (0, 1), (0, 2), (1, 1), (1, 2),
    (2, 1), (2, 2), (3, 1), (3, 2), (4, 1), (4, 2), (5, 1), (5, 2), (6, 1), (6, 2), (7, 1), (7, 2),
    (0, 3), (1, 3), (2, 3), (3, 3), (4, 3), (5, 3), (6, 3), (7, 3), (0, 4), (1, 4), (2, 4), (3, 4),
    (4, 4), (5, 4), (6, 4), (7, 4), (0, 5), (1, 5), (2, 5), (3, 5), (4, 5), (5, 5), (6, 5), (7, 5),
    (0, 6), (1, 6), (2, 6), (3, 6), (4, 6), (5, 6), (6, 6), (7, 6), (0, 7), (0, 8), (1, 7), (1, 8),
    (2, 7), (2, 8), (3, 7), (3, 8), (4, 7), (4, 8), (5, 7), (5, 8), (6, 7), (6, 8), (7, 7), (7, 8),
    (0, 9), (1, 9), (2, 9), (3, 9), (4, 9), (5, 9), (6, 9), (7, 9),
)


def dot(a, b, dims=((1,), (0,))):
    return lax.dot_general(a, b, (dims, ((), ())), preferred_element_type=F32)


def sigmoid(v):
    return 0.5 + 0.5 * jnp.tanh(0.5 * v)


def kernel(
    sizes, order,
    ids_ref, len_ref, table_hbm, basis_hbm, down_hbm, up_hbm, dcoef_hbm, out_hbm,
    table, basis, down, up, emb, emb_t, part, res,
    acc_s, acc_e, counts, gram, shared, turned, chain, own_e, all_e,
    z_st, xb_st, r_st, c_out, d_out, c_in, d_in, small, fb_st, e2_st, hop_out, hop_in,
    big_in, mids, mid_in, z_in,
    load_sem, mu_s, mu_r, e_s, e_r, c_s, c_r, d_s, d_r, hop_s, hop_r, ar_s, ar_r, st_sem,
):
    sections = lax.axis_size("section")
    group = all_e.shape[0]
    me = lax.axis_index("section")
    dp = lax.axis_index("dp")
    zh = lax.rem(dp, 2)
    cx = lax.rem(dp // 2, RING)
    cy = dp // (2 * RING)
    width, rank = basis.shape
    rows = emb.shape[0]
    mine = rows // group
    tiles = load_sem.shape[1]
    tile = width // tiles
    side = me // group
    here = lax.rem(me, group)
    partner = lax.rem(me + group, sections)

    def copy_to(src, dst, ssem, rsem, where):
        return pltpu.make_async_remote_copy(
            src_ref=src, dst_ref=dst, send_sem=ssem, recv_sem=rsem,
            device_id=where, device_id_type=MESH,
        )

    def others():
        for off in range(1, group):
            yield lax.rem(here + off, group)

    def device(t):
        return {"section": side * group + t}

    def at(x, y, z):
        return {"dp": (y * RING + x) * 2 + z}

    def turn(v, k):
        return lax.rem(v + k, RING)

    def load(n, i):
        src = (basis_hbm, down_hbm, up_hbm, table_hbm)[n]
        dst = (basis, down, up, table)[n]
        sl = pl.ds(pl.multiple_of(i * tile, tile), tile)
        if n == 3:
            return pltpu.make_async_copy(src.at[:, sl], dst.at[:, sl], load_sem.at[n, i])
        return pltpu.make_async_copy(src.at[sl, :], dst.at[sl, :], load_sem.at[n, i])

    for i in range(tiles):
        for n in range(3):
            load(n, i).start()
    for i in range(tiles):
        load(3, i).start()

    barrier = pltpu.get_barrier_semaphore()
    mates = [device(t) for t in others()] + [{"section": partner}]
    mates += [at(turn(cx, k), cy, zh) for k in range(1, RING)]
    mates += [at(cx, turn(cy, k), zh) for k in range(1, RING)]
    mates += [at(cx, cy, 1 - zh)]
    for mate in mates:
        pl.semaphore_signal(barrier, inc=1, device_id=mate, device_id_type=MESH)

    acc_s[...] = jnp.zeros_like(acc_s)

    @pl.loop(0, tiles)
    def _(i):
        for n in range(3):
            load(n, i).wait()
        sl = pl.ds(pl.multiple_of(i * tile, tile), tile)
        bt = basis[sl, :].T
        acc_s[0] += dot(bt, basis[sl, :])
        acc_s[1] += dot(bt, down[sl, :])
        acc_s[2] += dot(bt, up[sl, :])

    gram[...] = acc_s[0].astype(BF16)
    shared[pl.ds(here, 1), 0] = acc_s[1].astype(BF16)[None]
    shared[pl.ds(here, 1), 1] = acc_s[2].T.astype(BF16)[None]

    pl.semaphore_wait(barrier, len(mates))

    twin = here + 1 - 2 * lax.rem(here, 2)
    far = lax.rem(here + 2, group)
    far_twin = lax.rem(twin + 2, group)

    def share(k, what, to):
        return copy_to(shared.at[what], shared.at[what], mu_s.at[k], mu_r.at[k], device(to))

    share(1, here, far).start()
    share(0, here, twin).start()

    batches, slots, here_rows = ids_ref.shape
    codes = lax.broadcasted_iota(jnp.int32, (table.shape[0], here_rows), 0)
    for m in range(batches):
        total = jnp.zeros(codes.shape, F32)
        for j in range(slots):
            live = jnp.where(len_ref[m : m + 1, :] > j, ids_ref[m, j : j + 1, :], -1)
            total += jnp.where(live == codes, 1.0, 0.0)
        total = total.T
        rs = slice(m * here_rows, (m + 1) * here_rows)
        counts[rs, :] = total.astype(BF16)
        small[rs, :] = lax.rsqrt(jnp.sum(total, axis=1, keepdims=True))
    acc_e[...] = jnp.zeros_like(acc_e)
    step = rows // 4

    @pl.loop(0, tiles)
    def _(i):
        load(3, i).wait()
        sl = pl.ds(pl.multiple_of(i * tile, tile), tile)
        for q in range(2):
            rs = slice(q * rows // 2, (q + 1) * rows // 2)
            pre = dot(counts[rs, :], table[:, sl]) * small[rs, :]
            anchor = (pre * sigmoid(pre)).astype(BF16)
            emb[rs, sl] = anchor
            acc_e[rs, :] += dot(anchor, down[sl, :])

    own_e[...] = acc_e[...].astype(BF16)

    def slot(t):
        return pl.ds(pl.multiple_of(t * mine, mine), mine)

    def give_e(t):
        return copy_to(own_e.at[slot(t)], all_e.at[here], e_s.at[t], e_r.at[here], device(t))

    for t in others():
        give_e(t).start()
    all_e[pl.ds(here, 1)] = own_e[slot(here), :][None]

    fb = jnp.zeros((mine, rank), F32)
    e2 = jnp.zeros((mine, 1), F32)
    for i in range(tiles):
        piece = emb[slot(here), i * tile : (i + 1) * tile]
        fb += dot(piece, basis[i * tile : (i + 1) * tile, :])
        wide = piece.astype(F32)
        e2 += jnp.sum(wide * wide, axis=1, keepdims=True)
    fb_st[...] = fb
    e2_st[...] = e2

    share(1, far, far).wait_recv()
    share(2, far, twin).start()

    def turn_weights():
        for s in range(group):
            for n in range(2):
                turned[s, n] = shared[s, n].T
        for s in range(group - 1):
            chain[s, 2] = dot(turned[s + 1, 0], turned[s, 1]).astype(BF16)

    def flip():
        @pl.loop(0, tiles)
        def _(i):
            sl = pl.ds(pl.multiple_of(i * tile, tile), tile)
            for q in range(4):
                rs = slice(q * step, (q + 1) * step)
                emb_t[sl, rs] = emb[rs, sl].T

    share(0, twin, twin).wait_recv()
    share(2, far_twin, twin).wait_recv()
    for s in range(group - 1):
        chain[s, 0] = dot(shared[s, 1], shared[s + 1, 0]).astype(BF16)
        chain[s, 1] = dot(shared[s, 1], gram[...]).astype(BF16)
    for t in others():
        copy_to(own_e.at[slot(t)], all_e.at[t], e_s.at[t], e_r.at[t], device(t)).wait_recv()

    part_rows = mine // HALVES

    def cut(k):
        return pl.ds(k * part_rows, part_rows)

    def sub_slot(t, k):
        return pl.ds(pl.multiple_of(t * mine + k * part_rows, part_rows), part_rows)

    def give(out, into, ssem, rsem, t, k, source):
        return copy_to(
            out.at[t, cut(k)], into.at[sub_slot(source, k)], ssem.at[t, k], rsem.at[source, k],
            device(t),
        )

    def give_c(t, k):
        return give(c_out, c_in, c_s, c_r, t, k, here)

    def give_d(t, k):
        return give(d_out, d_in, d_s, d_r, t, k, here)

    def hop(n, k):
        return copy_to(
            hop_out.at[n, cut(k)], hop_in.at[n, cut(k)], hop_s.at[n, k], hop_r.at[n, k],
            {"section": partner},
        )

    inv = 1.0 / width

    def up_part(k, coef):
        fb, e2 = fb_st[cut(k), :], e2_st[cut(k), :]

        cg = cm = None
        for s in range(group):
            cb = coef.astype(BF16)
            c_out[s, cut(k)] = cb
            if s == 0:
                cg = dot(cb, gram[...])
                cm = dot(cb, shared[0, 0])
            xb = fb + cg
            sq = e2 + jnp.sum(coef * (fb + xb), axis=1, keepdims=True)
            r = lax.rsqrt(jnp.maximum(sq, 0.0) * inv + 1e-06)
            z = r * (all_e[s, cut(k)].astype(F32) + cm)
            z_st[s, cut(k)] = z
            xb_st[s, cut(k)] = xb
            r_st[s, cut(k)] = r
            act = (z * sigmoid(z)).astype(BF16)
            if s < group - 1:
                cm = dot(cb, shared[s + 1, 0]) + dot(act, chain[s, 0])
                cg = cg + dot(act, chain[s, 1])
            coef = coef + dot(act, shared[s, 1])
        return coef

    def down_part(k, grad, then):
        da = dot(grad.astype(BF16), turned[group - 1, 1])
        for s in reversed(range(group)):
            z = z_st[s, cut(k)]
            r = r_st[s, cut(k)]
            sig = sigmoid(z)
            dz = da * (sig * (1.0 + z * (1.0 - sig)))
            d_out[s, cut(k)] = (r * dz).astype(BF16)
            then(s)
            dzb = dz.astype(BF16)
            mean = jnp.sum(dz * z, axis=1, keepdims=True) * inv
            if s > 0:
                da = dot(grad.astype(BF16), turned[s - 1, 1]) + r * (
                    dot(dzb, chain[s - 1, 2])
                    - (r * mean) * dot(xb_st[s, cut(k)].astype(BF16), turned[s - 1, 1])
                )
            grad = grad + r * (dot(dzb, turned[s, 0]) - (r * mean) * xb_st[s, cut(k)])
        return grad

    @pl.when(side == 0)
    def _():
        for k in range(HALVES):
            coef = up_part(k, jnp.zeros((part_rows, rank), F32))
            hop_out[0, cut(k)] = coef.astype(BF16)
            hop(0, k).start()
        for t in others():
            for k in range(HALVES):
                give_c(t, k).start()
        turn_weights()
        flip()
        for k in range(HALVES):
            hop(1, k).wait_recv()

            def send_on(s):
                @pl.when(here != s)
                def _():
                    give_d(s, k).start()

            down_part(k, hop_in[1, cut(k)].astype(F32), send_on)

    @pl.when(side == 1)
    def _():
        last = pltpu.make_async_copy(dcoef_hbm.at[slot(here)], hop_in.at[1], st_sem.at[0])
        last.start()
        turn_weights()
        last.wait()
        for k in range(HALVES):
            hop(0, k).wait_recv()
            up_part(k, hop_in[0, cut(k)].astype(F32))
            grad = down_part(k, hop_in[1, cut(k)].astype(F32), lambda s: None)
            hop_out[1, cut(k)] = grad.astype(BF16)
            hop(1, k).start()
        for t in others():
            for k in range(HALVES):
                give_c(t, k).start()
                give_d(t, k).start()
        flip()

    c_in[slot(here), :] = c_out[pl.ds(here, 1)][0]
    d_in[slot(here), :] = d_out[pl.ds(here, 1)][0]
    for t in others():
        for k in range(HALVES):
            give(c_out, c_in, c_s, c_r, t, k, t).wait_recv()
            give(d_out, d_in, d_s, d_r, t, k, t).wait_recv()

    def clean():
        share(1, here, far).wait_send()
        share(0, here, twin).wait_send()
        share(2, far, twin).wait_send()
        for t in others():
            give_e(t).wait_send()
            for k in range(HALVES):
                give_c(t, k).wait_send()
                give_d(t, k).wait_send()

        @pl.when(side == 0)
        def _():
            for k in range(HALVES):
                hop(0, k).wait_send()

        @pl.when(side == 1)
        def _():
            for k in range(HALVES):
                hop(1, k).wait_send()

    gram[...] = dot(c_in[...].T, d_in[...]).astype(BF16)
    per = 17

    def rows_at(start, size):
        return pl.ds(pl.multiple_of(start, size), size)

    def along(st, stage, v):
        if st % 2 == stage:
            return at(v, cy, zh)
        return at(cx, v, zh)

    def add(*parts):
        total_ = parts[0].astype(F32)
        for p in parts[1:]:
            total_ += p.astype(F32)
        return total_.astype(BF16)

    def stream(st):
        own = sizes[st]
        base = sum(sizes[:st])
        b1, b2 = own // RING, own // RING // RING
        hf = b1 // 2
        big = big_in.at[pl.ds(base * 3 // 4, own * 3 // 4)]
        mid = mids.at[pl.ds(base * 5 // 16, own * 5 // 16)]
        subs = mid_in.at[pl.ds(base * 3 // 16, own * 3 // 16)]
        zin = z_in.at[pl.ds(base // 16, b2)]
        pos, pos2 = (cx, cy) if st % 2 == 0 else (cy, cx)
        right, left, opposite = turn(pos, 1), turn(pos, 3), turn(pos, 2)
        n0 = st * per

        def send(k, src, dst, to):
            return copy_to(src, dst, ar_s.at[n0 + k], ar_r.at[n0 + k], to)

        def blk(owner, part_no):
            return rows_at(base + owner * b1 + part_no * hf, hf)

        def over(k, owner, part_no, to):
            return send(k, part.at[blk(owner, part_no)], big.at[pl.ds(k * hf, hf)], along(st, 0, to))

        scat = [
            over(0, opposite, 0, right), over(1, opposite, 1, left), over(2, right, 1, right),
            over(3, left, 0, left), over(4, right, 0, right), over(5, left, 1, left),
        ]

        def sub(v):
            return rows_at(v * b2, b2)

        scat2 = [
            send(5 + o, mid.at[sub(turn(pos2, o))], subs.at[pl.ds((o - 1) * b2, b2)],
                 along(st, 1, turn(pos2, o)))
            for o in range(1, RING)
        ]
        swap = send(9, mid.at[pl.ds(b1, b2)], zin, at(cx, cy, 1 - zh))
        mine_sl = rows_at(base + pos * b1 + pos2 * b2, b2)
        gath2 = [
            send(9 + o, res.at[mine_sl], res.at[mine_sl], along(st, 1, turn(pos2, o)))
            for o in range(1, RING)
        ]

        def whole(k, owner, off, n, to):
            sl = rows_at(base + owner * b1 + off, n)
            return send(13 + k, res.at[sl], res.at[sl], along(st, 0, to))

        gath = [
            whole(0, pos, 0, b1, right), whole(1, pos, 0, b1, left),
            whole(2, left, 0, hf, right), whole(3, right, hf, hf, left),
        ]
        store = pltpu.make_async_copy(
            res.at[pl.ds(base, own)], out_hbm.at[pl.ds(base, own)], st_sem.at[st]
        )

        def product():
            @pl.loop(0, own // PR)
            def _(i):
                sl = rows_at(base + i * PR, PR)
                value = dot(emb_t[sl, :], d_in[...]) + dot(basis[sl, :], gram[...])
                part[sl, :] = value.astype(BF16)

            for k in range(4):
                scat[k].start()

        def pass_right():
            scat[0].wait_recv()
            part[blk(right, 0), :] = add(part[blk(right, 0), :], big[0 * hf : 1 * hf, :])
            scat[4].start()

        def pass_left():
            scat[1].wait_recv()
            part[blk(left, 1), :] = add(part[blk(left, 1), :], big[1 * hf : 2 * hf, :])
            scat[5].start()

        def block_done():
            scat[3].wait_recv()
            scat[4].wait_recv()
            mid[0:hf, :] = add(part[blk(pos, 0), :], big[3 * hf : 4 * hf, :], big[4 * hf : 5 * hf, :])
            scat[2].wait_recv()
            scat[5].wait_recv()
            mid[hf:b1, :] = add(part[blk(pos, 1), :], big[2 * hf : 3 * hf, :], big[5 * hf : 6 * hf, :])
            for m in scat2:
                m.start()

        def sub_done():
            for m in scat2:
                m.wait_recv()
            mid[b1 : b1 + b2, :] = add(
                mid[sub(pos2), :], subs[0 * b2 : 1 * b2, :], subs[1 * b2 : 2 * b2, :], subs[2 * b2 : 3 * b2, :]
            )
            swap.start()
            for m in scat:
                m.wait_send()

        def total_done():
            swap.wait_recv()
            res[mine_sl, :] = add(mid[b1 : b1 + b2, :], zin[...])
            for m in gath2:
                m.start()

        def block_back():
            for m in gath2:
                m.wait_recv()
            gath[0].start()
            gath[1].start()
            for m in scat2 + [swap] + gath2:
                m.wait_send()

        def forward_right():
            gath[0].wait_recv()
            gath[2].start()

        def forward_left():
            gath[1].wait_recv()
            gath[3].start()

        def out():
            gath[2].wait_recv()
            gath[3].wait_recv()
            store.start()

        def finish():
            for m in gath:
                m.wait_send()
            store.wait()

        stages = [
            product, pass_right, pass_left, block_done, sub_done, total_done, block_back,
            forward_right, forward_left, out,
        ]
        return stages, finish

    streams = len(sizes)
    made = [stream(st) for st in range(streams)]
    for n, (st, k) in enumerate(order):
        if n == streams:
            clean()
        made[st][0][k]()
    for st in range(streams):
        made[st][1]()


def place(src, dst, hold, sem):
    parts = sem.shape[1]
    n = src.shape[0] // parts
    cut = [pl.ds(i * n, n) for i in range(parts)]
    ins = [pltpu.make_async_copy(src.at[c], hold.at[c], sem.at[0, i]) for i, c in enumerate(cut)]
    outs = [pltpu.make_async_copy(hold.at[c], dst.at[c], sem.at[1, i]) for i, c in enumerate(cut)]
    for m in ins:
        m.start()
    for m, o in zip(ins, outs):
        m.wait()
        o.start()
    for o in outs:
        o.wait()


def on_device(byte_ids, patch_len, table, basis, w_down, w_up, dcoef):
    sections = lax.axis_size("section")
    batches, here, _ = byte_ids.shape
    rows = batches * here
    width, rank = basis.shape
    hidden = w_down.shape[2]
    group = sections // 2
    mine = rows // group
    tiles = 8
    sizes = SIZES
    streams = len(sizes)
    ids = jnp.transpose(byte_ids, (0, 2, 1))
    vmem = pl.BlockSpec(memory_space=pltpu.VMEM)
    hbm = pl.BlockSpec(memory_space=pl.ANY)
    dma = pltpu.SemaphoreType.DMA
    scratch = [
        pltpu.VMEM((table.shape[0], width), BF16),
        pltpu.VMEM((width, rank), BF16),
        pltpu.VMEM((width, hidden), BF16),
        pltpu.VMEM((width, hidden), BF16),
        pltpu.VMEM((rows, width), BF16),
        pltpu.VMEM((width, rows), BF16),
        pltpu.VMEM((width, hidden), BF16),
        pltpu.VMEM((width, hidden), BF16),
        pltpu.VMEM((3, rank, hidden), F32),
        pltpu.VMEM((rows, hidden), F32),
        pltpu.VMEM((rows, table.shape[0]), BF16),
        pltpu.VMEM((rank, hidden), BF16),
        pltpu.VMEM((group, 2, rank, hidden), BF16),
        pltpu.VMEM((group, 2, hidden, rank), BF16),
        pltpu.VMEM((group - 1, 3, hidden, hidden), BF16),
        pltpu.VMEM((rows, hidden), BF16),
        pltpu.VMEM((group, mine, hidden), BF16),
        pltpu.VMEM((group, mine, hidden), F32),
        pltpu.VMEM((group, mine, rank), F32),
        pltpu.VMEM((group, mine, 1), F32),
        pltpu.VMEM((group, mine, rank), BF16),
        pltpu.VMEM((group, mine, hidden), BF16),
        pltpu.VMEM((rows, rank), BF16),
        pltpu.VMEM((rows, hidden), BF16),
        pltpu.VMEM((rows, 1), F32),
        pltpu.VMEM((mine, rank), F32),
        pltpu.VMEM((mine, 1), F32),
        pltpu.VMEM((2, mine, rank), BF16),
        pltpu.VMEM((2, mine, rank), BF16),
        pltpu.VMEM((width * 3 // 4, hidden), BF16),
        pltpu.VMEM((width * 5 // 16, hidden), BF16),
        pltpu.VMEM((width * 3 // 16, hidden), BF16),
        pltpu.VMEM((width // 16, hidden), BF16),
        dma((4, tiles)), dma((3,)), dma((3,)),
        dma((group,)), dma((group,)), dma((group, HALVES)), dma((group, HALVES)),
        dma((group, HALVES)), dma((group, HALVES)), dma((2, HALVES)), dma((2, HALVES)), dma((streams * 17,)), dma((streams * 17,)), dma((streams,)),
    ]
    out = pl.pallas_call(
        functools.partial(kernel, sizes, ORDER),
        out_shape=jax.ShapeDtypeStruct((width, hidden), BF16),
        in_specs=[vmem, vmem, hbm, hbm, hbm, hbm, hbm],
        out_specs=hbm,
        scratch_shapes=scratch,
        compiler_params=pltpu.CompilerParams(
            collective_id=0, has_side_effects=True, vmem_limit_bytes=56 * 1024 * 1024
        ),
    )(ids, patch_len, table, basis, w_down[0], w_up[0], dcoef.reshape(rows, rank))
    out = pl.pallas_call(
        place,
        out_shape=jax.ShapeDtypeStruct((width, hidden), BF16),
        in_specs=[hbm],
        out_specs=hbm,
        scratch_shapes=[pltpu.VMEM((width, hidden), BF16), dma((2, 4))],
    )(out)
    return out[None]


def solution(mesh):
    return jax.shard_map(
        on_device,
        mesh=mesh,
        in_specs=(
            P(None, "dp", None),
            P(None, "dp"),
            P(),
            P(),
            P("section", None, None),
            P("section", None, None),
            P(None, "dp", None),
        ),
        out_specs=P("section", None, None),
        check_vma=False,
    )
```

```python
import functools

import jax
import jax.numpy as jnp
from jax import lax
from jax.experimental import pallas as pl
from jax.experimental.pallas import tpu as pltpu
from jax.sharding import PartitionSpec as P

MESH = pl.DeviceIdType.MESH
RING = 4
F32, BF16 = jnp.float32, jnp.bfloat16
HALVES = 1
PR = 512
SIZES = (512,) * 8
ORDER = (
    (0, 0), (1, 0), (2, 0), (3, 0), (4, 0), (5, 0), (6, 0), (7, 0), (0, 1), (0, 2), (1, 1), (1, 2),
    (2, 1), (2, 2), (3, 1), (3, 2), (4, 1), (4, 2), (5, 1), (5, 2), (6, 1), (6, 2), (7, 1), (7, 2),
    (0, 3), (1, 3), (2, 3), (3, 3), (4, 3), (5, 3), (6, 3), (7, 3), (0, 4), (1, 4), (2, 4), (3, 4),
    (4, 4), (5, 4), (6, 4), (7, 4), (0, 5), (1, 5), (2, 5), (3, 5), (4, 5), (5, 5), (6, 5), (7, 5),
    (0, 6), (1, 6), (2, 6), (3, 6), (4, 6), (5, 6), (6, 6), (7, 6), (0, 7), (0, 8), (1, 7), (1, 8),
    (2, 7), (2, 8), (3, 7), (3, 8), (4, 7), (4, 8), (5, 7), (5, 8), (6, 7), (6, 8), (7, 7), (7, 8),
    (0, 9), (1, 9), (2, 9), (3, 9), (4, 9), (5, 9), (6, 9), (7, 9),
)


def dot(a, b, dims=((1,), (0,))):
    return lax.dot_general(a, b, (dims, ((), ())), preferred_element_type=F32)


def sigmoid(v):
    return 0.5 + 0.5 * jnp.tanh(0.5 * v)


def kernel(
    sizes, order,
    ids_ref, len_ref, table_hbm, basis_hbm, down_hbm, up_hbm, dcoef_hbm, out_hbm,
    table, basis, down, up, emb, emb_t, part, res,
    acc_s, acc_e, counts, gram, shared, turned, chain, own_e, all_e,
    z_st, xb_st, r_st, c_out, d_out, c_in, d_in, small, fb_st, e2_st, hop_out, hop_in,
    big_in, mids, mid_in, z_in,
    load_sem, mu_s, mu_r, e_s, e_r, c_s, c_r, d_s, d_r, hop_s, hop_r, ar_s, ar_r, st_sem,
):
    sections = lax.axis_size("section")
    group = all_e.shape[0]
    me = lax.axis_index("section")
    dp = lax.axis_index("dp")
    zh = lax.rem(dp, 2)
    cx = lax.rem(dp // 2, RING)
    cy = dp // (2 * RING)
    width, rank = basis.shape
    rows = emb.shape[0]
    mine = rows // group
    tiles = load_sem.shape[1]
    tile = width // tiles
    side = me // group
    here = lax.rem(me, group)
    partner = lax.rem(me + group, sections)

    def copy_to(src, dst, ssem, rsem, where):
        return pltpu.make_async_remote_copy(
            src_ref=src, dst_ref=dst, send_sem=ssem, recv_sem=rsem,
            device_id=where, device_id_type=MESH,
        )

    def others():
        for off in range(1, group):
            yield lax.rem(here + off, group)

    def device(t):
        return {"section": side * group + t}

    def at(x, y, z):
        return {"dp": (y * RING + x) * 2 + z}

    def turn(v, k):
        return lax.rem(v + k, RING)

    def load(n, i):
        src = (basis_hbm, down_hbm, up_hbm, table_hbm)[n]
        dst = (basis, down, up, table)[n]
        sl = pl.ds(pl.multiple_of(i * tile, tile), tile)
        if n == 3:
            return pltpu.make_async_copy(src.at[:, sl], dst.at[:, sl], load_sem.at[n, i])
        return pltpu.make_async_copy(src.at[sl, :], dst.at[sl, :], load_sem.at[n, i])

    for i in range(tiles):
        for n in range(3):
            load(n, i).start()
    for i in range(tiles):
        load(3, i).start()

    barrier = pltpu.get_barrier_semaphore()
    mates = [device(t) for t in others()] + [{"section": partner}]
    mates += [at(turn(cx, k), cy, zh) for k in range(1, RING)]
    mates += [at(cx, turn(cy, k), zh) for k in range(1, RING)]
    mates += [at(cx, cy, 1 - zh)]
    for mate in mates:
        pl.semaphore_signal(barrier, inc=1, device_id=mate, device_id_type=MESH)

    acc_s[...] = jnp.zeros_like(acc_s)

    @pl.loop(0, tiles)
    def _(i):
        for n in range(3):
            load(n, i).wait()
        sl = pl.ds(pl.multiple_of(i * tile, tile), tile)
        bt = basis[sl, :].T
        acc_s[0] += dot(bt, basis[sl, :])
        acc_s[1] += dot(bt, down[sl, :])
        acc_s[2] += dot(bt, up[sl, :])

    gram[...] = acc_s[0].astype(BF16)
    shared[pl.ds(here, 1), 0] = acc_s[1].astype(BF16)[None]
    shared[pl.ds(here, 1), 1] = acc_s[2].T.astype(BF16)[None]

    pl.semaphore_wait(barrier, len(mates))

    twin = here + 1 - 2 * lax.rem(here, 2)
    far = lax.rem(here + 2, group)
    far_twin = lax.rem(twin + 2, group)

    def share(k, what, to):
        return copy_to(shared.at[what], shared.at[what], mu_s.at[k], mu_r.at[k], device(to))

    share(1, here, far).start()
    share(0, here, twin).start()

    batches, slots, here_rows = ids_ref.shape
    codes = lax.broadcasted_iota(jnp.int32, (table.shape[0], here_rows), 0)
    for m in range(batches):
        total = jnp.zeros(codes.shape, F32)
        for j in range(slots):
            live = jnp.where(len_ref[m : m + 1, :] > j, ids_ref[m, j : j + 1, :], -1)
            total += jnp.where(live == codes, 1.0, 0.0)
        total = total.T
        rs = slice(m * here_rows, (m + 1) * here_rows)
        counts[rs, :] = total.astype(BF16)
        small[rs, :] = lax.rsqrt(jnp.sum(total, axis=1, keepdims=True))
    acc_e[...] = jnp.zeros_like(acc_e)
    step = rows // 4

    @pl.loop(0, tiles)
    def _(i):
        load(3, i).wait()
        sl = pl.ds(pl.multiple_of(i * tile, tile), tile)
        for q in range(2):
            rs = slice(q * rows // 2, (q + 1) * rows // 2)
            pre = dot(counts[rs, :], table[:, sl]) * small[rs, :]
            anchor = (pre * sigmoid(pre)).astype(BF16)
            emb[rs, sl] = anchor
            acc_e[rs, :] += dot(anchor, down[sl, :])

    own_e[...] = acc_e[...].astype(BF16)

    def slot(t):
        return pl.ds(pl.multiple_of(t * mine, mine), mine)

    def give_e(t):
        return copy_to(own_e.at[slot(t)], all_e.at[here], e_s.at[t], e_r.at[here], device(t))

    for t in others():
        give_e(t).start()
    all_e[pl.ds(here, 1)] = own_e[slot(here), :][None]

    fb = jnp.zeros((mine, rank), F32)
    e2 = jnp.zeros((mine, 1), F32)
    for i in range(tiles):
        piece = emb[slot(here), i * tile : (i + 1) * tile]
        fb += dot(piece, basis[i * tile : (i + 1) * tile, :])
        wide = piece.astype(F32)
        e2 += jnp.sum(wide * wide, axis=1, keepdims=True)
    fb_st[...] = fb
    e2_st[...] = e2

    share(1, far, far).wait_recv()
    share(2, far, twin).start()

    def turn_weights():
        for s in range(group):
            for n in range(2):
                turned[s, n] = shared[s, n].T
        for s in range(group - 1):
            chain[s, 2] = dot(turned[s + 1, 0], turned[s, 1]).astype(BF16)

    def flip():
        @pl.loop(0, tiles)
        def _(i):
            sl = pl.ds(pl.multiple_of(i * tile, tile), tile)
            for q in range(4):
                rs = slice(q * step, (q + 1) * step)
                emb_t[sl, rs] = emb[rs, sl].T

    share(0, twin, twin).wait_recv()
    share(2, far_twin, twin).wait_recv()
    for s in range(group - 1):
        chain[s, 0] = dot(shared[s, 1], shared[s + 1, 0]).astype(BF16)
        chain[s, 1] = dot(shared[s, 1], gram[...]).astype(BF16)
    for t in others():
        copy_to(own_e.at[slot(t)], all_e.at[t], e_s.at[t], e_r.at[t], device(t)).wait_recv()

    part_rows = mine // HALVES

    def cut(k):
        return pl.ds(k * part_rows, part_rows)

    def sub_slot(t, k):
        return pl.ds(pl.multiple_of(t * mine + k * part_rows, part_rows), part_rows)

    def give(out, into, ssem, rsem, t, k, source):
        return copy_to(
            out.at[t, cut(k)], into.at[sub_slot(source, k)], ssem.at[t, k], rsem.at[source, k],
            device(t),
        )

    def give_c(t, k):
        return give(c_out, c_in, c_s, c_r, t, k, here)

    def give_d(t, k):
        return give(d_out, d_in, d_s, d_r, t, k, here)

    def hop(n, k):
        return copy_to(
            hop_out.at[n, cut(k)], hop_in.at[n, cut(k)], hop_s.at[n, k], hop_r.at[n, k],
            {"section": partner},
        )

    inv = 1.0 / width

    def up_part(k, coef):
        fb, e2 = fb_st[cut(k), :], e2_st[cut(k), :]

        cg = cm = None
        for s in range(group):
            cb = coef.astype(BF16)
            c_out[s, cut(k)] = cb
            if s == 0:
                cg = dot(cb, gram[...])
                cm = dot(cb, shared[0, 0])
            xb = fb + cg
            sq = e2 + jnp.sum(coef * (fb + xb), axis=1, keepdims=True)
            r = lax.rsqrt(jnp.maximum(sq, 0.0) * inv + 1e-06)
            z = r * (all_e[s, cut(k)].astype(F32) + cm)
            z_st[s, cut(k)] = z
            xb_st[s, cut(k)] = xb
            r_st[s, cut(k)] = r
            act = (z * sigmoid(z)).astype(BF16)
            if s < group - 1:
                cm = dot(cb, shared[s + 1, 0]) + dot(act, chain[s, 0])
                cg = cg + dot(act, chain[s, 1])
            coef = coef + dot(act, shared[s, 1])
        return coef

    def down_part(k, grad, then):
        da = dot(grad.astype(BF16), turned[group - 1, 1])
        for s in reversed(range(group)):
            z = z_st[s, cut(k)]
            r = r_st[s, cut(k)]
            sig = sigmoid(z)
            dz = da * (sig * (1.0 + z * (1.0 - sig)))
            d_out[s, cut(k)] = (r * dz).astype(BF16)
            then(s)
            dzb = dz.astype(BF16)
            mean = jnp.sum(dz * z, axis=1, keepdims=True) * inv
            if s > 0:
                da = dot(grad.astype(BF16), turned[s - 1, 1]) + r * (
                    dot(dzb, chain[s - 1, 2])
                    - (r * mean) * dot(xb_st[s, cut(k)].astype(BF16), turned[s - 1, 1])
                )
            grad = grad + r * (dot(dzb, turned[s, 0]) - (r * mean) * xb_st[s, cut(k)])
        return grad

    @pl.when(side == 0)
    def _():
        for k in range(HALVES):
            coef = up_part(k, jnp.zeros((part_rows, rank), F32))
            hop_out[0, cut(k)] = coef.astype(BF16)
            hop(0, k).start()
        for t in others():
            for k in range(HALVES):
                give_c(t, k).start()
        turn_weights()
        flip()
        for k in range(HALVES):
            hop(1, k).wait_recv()

            def send_on(s):
                @pl.when(here != s)
                def _():
                    give_d(s, k).start()

            down_part(k, hop_in[1, cut(k)].astype(F32), send_on)

    @pl.when(side == 1)
    def _():
        last = pltpu.make_async_copy(dcoef_hbm.at[slot(here)], hop_in.at[1], st_sem.at[0])
        last.start()
        turn_weights()
        last.wait()
        for k in range(HALVES):
            hop(0, k).wait_recv()
            up_part(k, hop_in[0, cut(k)].astype(F32))
            grad = down_part(k, hop_in[1, cut(k)].astype(F32), lambda s: None)
            hop_out[1, cut(k)] = grad.astype(BF16)
            hop(1, k).start()
        for t in others():
            for k in range(HALVES):
                give_c(t, k).start()
                give_d(t, k).start()
        flip()

    c_in[slot(here), :] = c_out[pl.ds(here, 1)][0]
    d_in[slot(here), :] = d_out[pl.ds(here, 1)][0]
    for t in others():
        for k in range(HALVES):
            give(c_out, c_in, c_s, c_r, t, k, t).wait_recv()
            give(d_out, d_in, d_s, d_r, t, k, t).wait_recv()

    def clean():
        share(1, here, far).wait_send()
        share(0, here, twin).wait_send()
        share(2, far, twin).wait_send()
        for t in others():
            give_e(t).wait_send()
            for k in range(HALVES):
                give_c(t, k).wait_send()
                give_d(t, k).wait_send()

        @pl.when(side == 0)
        def _():
            for k in range(HALVES):
                hop(0, k).wait_send()

        @pl.when(side == 1)
        def _():
            for k in range(HALVES):
                hop(1, k).wait_send()

    gram[...] = dot(c_in[...].T, d_in[...]).astype(BF16)
    per = 17

    def rows_at(start, size):
        return pl.ds(pl.multiple_of(start, size), size)

    def along(st, stage, v):
        if st % 2 == stage:
            return at(v, cy, zh)
        return at(cx, v, zh)

    def add(*parts):
        total_ = parts[0].astype(F32)
        for p in parts[1:]:
            total_ += p.astype(F32)
        return total_.astype(BF16)

    def stream(st):
        own = sizes[st]
        base = sum(sizes[:st])
        b1, b2 = own // RING, own // RING // RING
        hf = b1 // 2
        big = big_in.at[pl.ds(base * 3 // 4, own * 3 // 4)]
        mid = mids.at[pl.ds(base * 5 // 16, own * 5 // 16)]
        subs = mid_in.at[pl.ds(base * 3 // 16, own * 3 // 16)]
        zin = z_in.at[pl.ds(base // 16, b2)]
        pos, pos2 = (cx, cy) if st % 2 == 0 else (cy, cx)
        right, left, opposite = turn(pos, 1), turn(pos, 3), turn(pos, 2)
        n0 = st * per

        def send(k, src, dst, to):
            return copy_to(src, dst, ar_s.at[n0 + k], ar_r.at[n0 + k], to)

        def blk(owner, part_no):
            return rows_at(base + owner * b1 + part_no * hf, hf)

        def over(k, owner, part_no, to):
            return send(k, part.at[blk(owner, part_no)], big.at[pl.ds(k * hf, hf)], along(st, 0, to))

        scat = [
            over(0, opposite, 0, right), over(1, opposite, 1, left), over(2, right, 1, right),
            over(3, left, 0, left), over(4, right, 0, right), over(5, left, 1, left),
        ]

        def sub(v):
            return rows_at(v * b2, b2)

        scat2 = [
            send(5 + o, mid.at[sub(turn(pos2, o))], subs.at[pl.ds((o - 1) * b2, b2)],
                 along(st, 1, turn(pos2, o)))
            for o in range(1, RING)
        ]
        swap = send(9, mid.at[pl.ds(b1, b2)], zin, at(cx, cy, 1 - zh))
        mine_sl = rows_at(base + pos * b1 + pos2 * b2, b2)
        gath2 = [
            send(9 + o, res.at[mine_sl], res.at[mine_sl], along(st, 1, turn(pos2, o)))
            for o in range(1, RING)
        ]

        def whole(k, owner, off, n, to):
            sl = rows_at(base + owner * b1 + off, n)
            return send(13 + k, res.at[sl], res.at[sl], along(st, 0, to))

        gath = [
            whole(0, pos, 0, b1, right), whole(1, pos, 0, b1, left),
            whole(2, left, 0, hf, right), whole(3, right, hf, hf, left),
        ]
        store = pltpu.make_async_copy(
            res.at[pl.ds(base, own)], out_hbm.at[pl.ds(base, own)], st_sem.at[st]
        )

        def product():
            @pl.loop(0, own // PR)
            def _(i):
                sl = rows_at(base + i * PR, PR)
                value = dot(emb_t[sl, :], d_in[...]) + dot(basis[sl, :], gram[...])
                part[sl, :] = value.astype(BF16)

            for k in range(4):
                scat[k].start()

        def pass_right():
            scat[0].wait_recv()
            part[blk(right, 0), :] = add(part[blk(right, 0), :], big[0 * hf : 1 * hf, :])
            scat[4].start()

        def pass_left():
            scat[1].wait_recv()
            part[blk(left, 1), :] = add(part[blk(left, 1), :], big[1 * hf : 2 * hf, :])
            scat[5].start()

        def block_done():
            scat[3].wait_recv()
            scat[4].wait_recv()
            mid[0:hf, :] = add(part[blk(pos, 0), :], big[3 * hf : 4 * hf, :], big[4 * hf : 5 * hf, :])
            scat[2].wait_recv()
            scat[5].wait_recv()
            mid[hf:b1, :] = add(part[blk(pos, 1), :], big[2 * hf : 3 * hf, :], big[5 * hf : 6 * hf, :])
            for m in scat2:
                m.start()

        def sub_done():
            for m in scat2:
                m.wait_recv()
            mid[b1 : b1 + b2, :] = add(
                mid[sub(pos2), :], subs[0 * b2 : 1 * b2, :], subs[1 * b2 : 2 * b2, :], subs[2 * b2 : 3 * b2, :]
            )
            swap.start()
            for m in scat:
                m.wait_send()

        def total_done():
            swap.wait_recv()
            res[mine_sl, :] = add(mid[b1 : b1 + b2, :], zin[...])
            for m in gath2:
                m.start()

        def block_back():
            for m in gath2:
                m.wait_recv()
            gath[0].start()
            gath[1].start()
            for m in scat2 + [swap] + gath2:
                m.wait_send()

        def forward_right():
            gath[0].wait_recv()
            gath[2].start()

        def forward_left():
            gath[1].wait_recv()
            gath[3].start()

        def out():
            gath[2].wait_recv()
            gath[3].wait_recv()
            store.start()

        def finish():
            for m in gath:
                m.wait_send()
            store.wait()

        stages = [
            product, pass_right, pass_left, block_done, sub_done, total_done, block_back,
            forward_right, forward_left, out,
        ]
        return stages, finish

    streams = len(sizes)
    made = [stream(st) for st in range(streams)]
    for n, (st, k) in enumerate(order):
        if n == streams:
            clean()
        made[st][0][k]()
    for st in range(streams):
        made[st][1]()


def place(src, dst, hold, sem):
    parts = sem.shape[1]
    n = src.shape[0] // parts
    cut = [pl.ds(i * n, n) for i in range(parts)]
    ins = [pltpu.make_async_copy(src.at[c], hold.at[c], sem.at[0, i]) for i, c in enumerate(cut)]
    outs = [pltpu.make_async_copy(hold.at[c], dst.at[c], sem.at[1, i]) for i, c in enumerate(cut)]
    for m in ins:
        m.start()
    for m, o in zip(ins, outs):
        m.wait()
        o.start()
    for o in outs:
        o.wait()


def on_device(byte_ids, patch_len, table, basis, w_down, w_up, dcoef):
    sections = lax.axis_size("section")
    batches, here, _ = byte_ids.shape
    rows = batches * here
    width, rank = basis.shape
    hidden = w_down.shape[2]
    group = sections // 2
    mine = rows // group
    tiles = 8
    sizes = SIZES
    streams = len(sizes)
    ids = jnp.transpose(byte_ids, (0, 2, 1))
    vmem = pl.BlockSpec(memory_space=pltpu.VMEM)
    hbm = pl.BlockSpec(memory_space=pl.ANY)
    dma = pltpu.SemaphoreType.DMA
    scratch = [
        pltpu.VMEM((table.shape[0], width), BF16),
        pltpu.VMEM((width, rank), BF16),
        pltpu.VMEM((width, hidden), BF16),
        pltpu.VMEM((width, hidden), BF16),
        pltpu.VMEM((rows, width), BF16),
        pltpu.VMEM((width, rows), BF16),
        pltpu.VMEM((width, hidden), BF16),
        pltpu.VMEM((width, hidden), BF16),
        pltpu.VMEM((3, rank, hidden), F32),
        pltpu.VMEM((rows, hidden), F32),
        pltpu.VMEM((rows, table.shape[0]), BF16),
        pltpu.VMEM((rank, hidden), BF16),
        pltpu.VMEM((group, 2, rank, hidden), BF16),
        pltpu.VMEM((group, 2, hidden, rank), BF16),
        pltpu.VMEM((group - 1, 3, hidden, hidden), BF16),
        pltpu.VMEM((rows, hidden), BF16),
        pltpu.VMEM((group, mine, hidden), BF16),
        pltpu.VMEM((group, mine, hidden), F32),
        pltpu.VMEM((group, mine, rank), F32),
        pltpu.VMEM((group, mine, 1), F32),
        pltpu.VMEM((group, mine, rank), BF16),
        pltpu.VMEM((group, mine, hidden), BF16),
        pltpu.VMEM((rows, rank), BF16),
        pltpu.VMEM((rows, hidden), BF16),
        pltpu.VMEM((rows, 1), F32),
        pltpu.VMEM((mine, rank), F32),
        pltpu.VMEM((mine, 1), F32),
        pltpu.VMEM((2, mine, rank), BF16),
        pltpu.VMEM((2, mine, rank), BF16),
        pltpu.VMEM((width * 3 // 4, hidden), BF16),
        pltpu.VMEM((width * 5 // 16, hidden), BF16),
        pltpu.VMEM((width * 3 // 16, hidden), BF16),
        pltpu.VMEM((width // 16, hidden), BF16),
        dma((4, tiles)), dma((3,)), dma((3,)),
        dma((group,)), dma((group,)), dma((group, HALVES)), dma((group, HALVES)),
        dma((group, HALVES)), dma((group, HALVES)), dma((2, HALVES)), dma((2, HALVES)), dma((streams * 17,)), dma((streams * 17,)), dma((streams,)),
    ]
    out = pl.pallas_call(
        functools.partial(kernel, sizes, ORDER),
        out_shape=jax.ShapeDtypeStruct((width, hidden), BF16),
        in_specs=[vmem, vmem, hbm, hbm, hbm, hbm, hbm],
        out_specs=hbm,
        scratch_shapes=scratch,
        compiler_params=pltpu.CompilerParams(
            collective_id=0, has_side_effects=True, vmem_limit_bytes=56 * 1024 * 1024
        ),
    )(ids, patch_len, table, basis, w_down[0], w_up[0], dcoef.reshape(rows, rank))
    out = pl.pallas_call(
        place,
        out_shape=jax.ShapeDtypeStruct((width, hidden), BF16),
        in_specs=[hbm],
        out_specs=hbm,
        scratch_shapes=[pltpu.VMEM((width, hidden), BF16), dma((2, 4))],
    )(out)
    return out[None]


def solution(mesh):
    return jax.shard_map(
        on_device,
        mesh=mesh,
        in_specs=(
            P(None, "dp", None),
            P(None, "dp"),
            P(),
            P(),
            P("section", None, None),
            P("section", None, None),
            P(None, "dp", None),
        ),
        out_specs=P("section", None, None),
        check_vma=False,
    )
```
